512 devices in a mesh: grp: 4 (over x), dom: 128 (over y, z, core).
Axes of the slice: x: 4, y: 8, z: 8, core: 2. Of those that a mesh axis runs over, the one named last changes fastest.
Arguments:
- positions: float32 [3, 2097152], P(None, ('grp', 'dom')), may hold values from -6 to 6
- velocities: float32 [3, 2097152], P(None, ('grp', 'dom')), may hold values from -6 to 6
- particle_volume: float32 [2097152], P(('grp', 'dom')), may hold values from 0.5 to 2
- drag_coef: float32 [2097152], P(('grp', 'dom')), may hold values from 0.2 to 5
- gas_at_particle: float32 [3, 2097152], P(None, ('grp', 'dom')), may hold values from -6 to 6
- pair_first: int32 [65536], P(('grp', 'dom')), may hold values from 0 to 31
- pair_second: int32 [65536], P(('grp', 'dom')), may hold values from 0 to 35
- ghost_list: int32 [2, 1024], P(None, ('grp', 'dom')), may hold values from 0 to 31
- block_owner: int32 [16384, 1], P(('grp', 'dom')), may hold values from 0 to 127; in each aligned block of 32 rows (0 to 31, 32 to 63, ...) at most 2 rows name the same one
- cell_map: int32 [2097152], P(('grp', 'dom')), may hold values from 0 to 511
- gas_velocity: float32 [3, 262144], P(None, ('grp', 'dom')), may hold values from -6 to 6
Outputs:
- positions_out: float32 [3, 2097152], P(None, ('grp', 'dom'))
- velocities_out: float32 [3, 2097152], P(None, ('grp', 'dom'))
- gas_out: float32 [3, 262144], P(None, ('grp', 'dom'))
- void_out: float32 [262144], P(('grp', 'dom'))
- particle_gas: float32 [3, 2097152], P(None, ('grp', 'dom'))
The draws below stay inside these ranges and needn't reach their ends.
Inputs may be any that keep to these rules, and one draw needn't show every extreme that they name: `block_owner`: in the 32 blocks of one device no owner is named by more than 2 blocks, a bound that some block reaches. `pair_second`: values 32 to 33 name ghosts from the previous device, the next 2 those from the next device.
All inputs are finite; a program needn't handle non-finite values.
Results may differ from the reference program's by a relative error of at most 0.0003.
Values sent between devices are 32-bit elements; how exact they have to be, the bound alone decides.
No kernel may reach another device: no remote copies, remote signals or barrier semaphores. Data moves between devices by JAX's collectives and lax.ppermute only.
A program may use at most 128 MiB of HBM per device.

```python
import math
import jax
import jax.numpy as jnp
import numpy as np
from jax import lax

NB = 32
BP = 128
C = 512
K = 5
SUBSTEPS = 4
SWEEPS = 4
NG = 2
NPAIR = 128
CAP = 2
PARTICLES = 2097152
BLOCKS = 16384
PAIRS = 65536
GHOSTS = 1024
CELLS = 262144
N_GRP = 4
N_DOM = 128


def touch_ends(entries, stream_key, low, largest):
    dims = entries.shape
    spot = [jax.random.randint(jax.random.fold_in(stream_key, axis), (), 0, dims[axis]) for axis in range(len(dims))]
    entries = entries.at[tuple(spot)].set(low)
    longest = dims.index(max(dims))
    spot[longest] = (spot[longest] + 1) % dims[longest]
    return entries.at[tuple(spot)].set(largest)


def block_scale(stream_key, extent, split, least, high):
    factor_of = 1.0
    for position, parts in split:
        draws = jax.random.uniform(jax.random.fold_in(jax.random.fold_in(stream_key, 6), position), (parts,), jnp.float32, least / len(split), high / len(split))
        factor_of = factor_of * jnp.repeat(jnp.exp(draws), extent[position] // parts).reshape((-1,) + (1,) * (len(extent) - 1 - position))
    return factor_of


def assign_block(key, own, number, rows, number_of, top, limit, skew):
    ranking = jax.random.permutation(key, number_of)
    heavy_load, common = portions_of(number_of, rows * top, limit, skew, True), portions_of(number_of, rows * top, limit, skew, False)
    places = jnp.arange(number_of)

    def named(lengths, turn):
        used = int((lengths > 0).sum())
        fixed = max(1, used // 4)
        passed = fixed + (places - fixed + turn * (used - fixed)) % max(1, number_of - fixed)
        return jnp.zeros((number_of,), jnp.int32).at[ranking[jnp.where(places < fixed, places, passed)]].set(jnp.asarray(lengths, jnp.int32))

    lengths = jnp.where(number % 4 == 0, named(heavy_load, number // 4), named(common, number - number // 4 - 1))
    mixed = jax.random.permutation(jax.random.fold_in(own, 3), number_of)
    donor, receiver = mixed[0:number_of // 2 * 2:2], mixed[1:number_of // 2 * 2:2]
    margin = jnp.minimum(lengths[donor] - 1, limit - lengths[receiver]) // 2
    margin = jnp.where((donor == ranking[0]) | (receiver == ranking[0]) | (lengths[receiver] == 0), 0, jnp.maximum(margin, 0))
    passed = jax.random.randint(jax.random.fold_in(own, 4), (number_of // 2,), 0, 1 << 20) % (margin + 1)
    lengths = lengths.at[donor].add(-passed).at[receiver].add(passed)
    members = jnp.searchsorted(jnp.cumsum(lengths), jnp.arange(rows * top), side="right").astype(jnp.int32)
    table = members.reshape(top, rows).T
    table = table[jax.random.permutation(jax.random.fold_in(own, 1), rows)]
    turn = jax.random.randint(jax.random.fold_in(own, 2), (rows, 1), 0, top)
    return jnp.take_along_axis(table, (jnp.arange(top)[None, :] + turn) % top, axis=1)


def portions_of(count, total, bound, slope, full):
    loads = [(1 << 20) // math.isqrt(grade ** slope) + 1 for grade in range(1, count + 1)]
    largest = bound if full else min(bound, max(-(-total // count), total * loads[0] // sum(loads)))
    least = 1 if total - largest >= count - 1 else 0
    given, spare = [largest] + [least] * (count - 1), total - largest - least * (count - 1)
    while spare > 0:
        free = [i for i in range(1, count) if given[i] < largest] or [i for i in range(1, count) if given[i] < bound]
        whole, remaining = sum([loads[i] for i in free]), spare
        for i in free:
            more = min(bound - given[i], max(1, remaining * loads[i] // whole), spare)
            given[i] = given[i] + more
            spare = spare - more
    return np.array(given)


def bell_draw(stream_key, dims, spread, most, cuts=(), kind=jnp.bfloat16):
    drawn = spread * jax.random.normal(stream_key, dims, jnp.float32)
    if cuts:
        drawn = drawn * block_scale(stream_key, dims, cuts, -0.22, 0.18)
    return jnp.clip(drawn, -most, most).astype(kind)


def setup_inputs(seed: int = 0) -> dict:
    key_of = jax.random.split(jax.random.key(seed), 12)
    positions = bell_draw(key_of[0], (3, PARTICLES), 1.5, 6.0, ((1, 512),), jnp.float32)
    velocities = bell_draw(key_of[1], (3, PARTICLES), 1.0, 6.0, ((1, 512),), jnp.float32)
    particle_volume = jnp.clip(jnp.exp(math.log(2.0) - 1.3862944 * jax.random.uniform(key_of[2], (PARTICLES,), jnp.float32) ** block_scale(key_of[2], (PARTICLES,), ((0, 512),), -0.2, 0.2)), 0.5, 2.0)
    drag_coef = jnp.clip(jnp.exp(math.log(5.0) - 3.218876 * jax.random.uniform(key_of[3], (PARTICLES,), jnp.float32) ** block_scale(key_of[3], (PARTICLES,), ((0, 512),), -0.2, 0.2)), 0.2, 5.0)
    gas_at_particle = bell_draw(key_of[4], (3, PARTICLES), 1.0, 6.0, ((1, 512),), jnp.float32)
    pair_first = touch_ends(jax.random.randint(key_of[5], (PAIRS,), 0, NB), jax.random.fold_in(key_of[5], 1), 0, NB - 1).astype(jnp.int32)
    pair_second = touch_ends(jax.random.randint(key_of[6], (PAIRS,), 0, NB + 2 * NG), jax.random.fold_in(key_of[6], 1), 0, (NB + 2 * NG) - 1).astype(jnp.int32)
    ghost_list = touch_ends(jax.random.randint(key_of[7], (2, GHOSTS), 0, NB), jax.random.fold_in(key_of[7], 1), 0, NB - 1).astype(jnp.int32)
    block_owner_keys = jax.random.split(jax.random.fold_in(key_of[8], 1), BLOCKS // NB)
    block_owner_turns = jax.random.permutation(jax.random.fold_in(key_of[8], 3), BLOCKS // NB)
    block_owner = jax.vmap(lambda own, number: assign_block(jax.random.fold_in(key_of[8], 2), own, number, NB, N_DOM, 1, CAP, 2))(block_owner_keys, block_owner_turns).reshape((BLOCKS, 1))
    cell_map = touch_ends(jax.random.randint(key_of[9], (PARTICLES,), 0, C), jax.random.fold_in(key_of[9], 1), 0, C - 1).astype(jnp.int32)
    gas_velocity = bell_draw(key_of[10], (3, CELLS), 1.0, 6.0, ((1, 512),), jnp.float32)
    return {"positions": positions, "velocities": velocities, "particle_volume": particle_volume, "drag_coef": drag_coef, "gas_at_particle": gas_at_particle, "pair_first": pair_first, "pair_second": pair_second, "ghost_list": ghost_list, "block_owner": block_owner, "cell_map": cell_map, "gas_velocity": gas_velocity}


SLAB = 4.0
SOFT = 0.01
STIFF = 20.0
NORMAL_DAMP = 2.0
TANGENT_DAMP = 1.0
STEP = 0.01
GRAVITY_Z = -1.0
RADIUS_FACTOR = 0.62
CELL_VOLUME = 16.0
RHO_STEP = 2.0
VISCOSITY = 1.0

def pair_force(xi, vi, ri, xj, vj, rj):
    delta_vec = xi[:, :, :, None] - xj[:, :, None, :]
    dist = jnp.sqrt(lax.optimization_barrier(jnp.sum(delta_vec * delta_vec, axis=0)) + SOFT)
    normal = delta_vec / dist[None]
    intersection = jnp.maximum(ri[:, :, None] + rj[:, None, :] - dist, 0.0)
    root = jnp.sqrt(intersection)
    relative = vi[:, :, :, None] - vj[:, :, None, :]
    speed_n = lax.optimization_barrier(jnp.sum(relative * normal, axis=0))
    push = STIFF * intersection * root - NORMAL_DAMP * root * speed_n
    force = push[None] * normal - TANGENT_DAMP * root[None] * (relative - speed_n[None] * normal)
    return lax.optimization_barrier(jnp.sum(force, axis=3))

def contact_forces(extended, first, second, nblocks):
    width = extended.shape[2]
    xi = extended[0:3][:, first]
    vi = extended[3:6][:, first]
    ri = extended[6][first]
    xj = extended[0:3][:, second]
    vj = extended[3:6][:, second]
    rj = extended[6][second]
    groups = first.shape[0] // 8

    def one_group(k):
        start = k * 8
        return pair_force(lax.dynamic_slice_in_dim(xi, start, 8, 1), lax.dynamic_slice_in_dim(vi, start, 8, 1), lax.dynamic_slice_in_dim(ri, start, 8, 0), lax.dynamic_slice_in_dim(xj, start, 8, 1), lax.dynamic_slice_in_dim(vj, start, 8, 1), lax.dynamic_slice_in_dim(rj, start, 8, 0))
    per_pair = lax.map(one_group, jnp.arange(groups, dtype=jnp.int32))
    per_pair = jnp.moveaxis(per_pair, 0, 1).reshape(3, groups * 8, width)
    onehot = (first[None, :] == jnp.arange(nblocks, dtype=jnp.int32)[:, None]).astype(jnp.float32)
    return jnp.einsum('bp,cpq->cbq', onehot, per_pair, precision=lax.Precision.HIGHEST)

def advance(pos, vel, force, gas_seen, beta, mass):
    gravity = jnp.array([0.0, 0.0, GRAVITY_Z], dtype=jnp.float32)[:, None, None]
    beta3 = jnp.expand_dims(beta, -3)
    mass3 = jnp.expand_dims(mass, -3)
    accel = (force + beta3 * (gas_seen - vel)) / mass3 + gravity
    vel = vel + STEP * accel
    pos = pos + STEP * vel
    return (pos, vel)

def reference(positions, velocities, particle_volume, drag_coef, gas_at_particle, pair_first, pair_second, ghost_list, block_owner, cell_map, gas_velocity):
    devices = N_GRP * N_DOM

    def blocks(a):
        return a.reshape(3, devices, NB, BP).transpose(1, 0, 2, 3)
    pos = blocks(positions)
    vel = blocks(velocities)
    gas_seen = blocks(gas_at_particle)
    mass = particle_volume.reshape(devices, NB, BP)
    beta = drag_coef.reshape(devices, NB, BP)
    radius = RADIUS_FACTOR * mass ** (1.0 / 3.0)
    first = pair_first.reshape(devices, NPAIR)
    second = pair_second.reshape(devices, NPAIR)
    ghosts = ghost_list.reshape(2, devices, NG)
    owner = block_owner.reshape(devices, NB)
    shift_vec = jnp.array([SLAB, 0.0, 0.0, 0.0, 0.0, 0.0, 0.0], dtype=jnp.float32)[:, None, None]
    pick = jax.vmap(lambda load, chosen: load[:, chosen])
    for step in range(SUBSTEPS):
        payload = jnp.concatenate([pos, vel, radius[:, None]], axis=1)
        below = jnp.roll(pick(payload, ghosts[0]), 1, axis=0) - shift_vec
        above = jnp.roll(pick(payload, ghosts[1]), -1, axis=0) + shift_vec
        extended = jnp.concatenate([payload, below, above], axis=2)
        force = lax.map(lambda item: contact_forces(item[0], item[1], item[2], NB), (extended, first, second))
        pos, vel = advance(pos, vel, force, gas_seen, beta, mass)
    quantities = jnp.concatenate([mass[:, None], beta[:, None], beta[:, None] * vel], axis=1)
    base = jnp.arange(devices, dtype=jnp.int32) // N_DOM * N_DOM
    target = base[:, None] + owner
    index = (target[:, :, None] * C + cell_map.reshape(devices, NB, BP)).reshape(-1).astype(jnp.int32)
    data = quantities.transpose(0, 2, 3, 1).reshape(-1, K)
    dep = jax.ops.segment_sum(data, index, num_segments=devices * C).T
    void_out = CELL_VOLUME / (CELL_VOLUME + dep[0])
    inertia = RHO_STEP * void_out
    drag_sum = dep[1] / CELL_VOLUME
    drag_mom = dep[2:5] / CELL_VOLUME
    diag = inertia + drag_sum + 2.0 * VISCOSITY
    known = inertia[None] * gas_velocity + drag_mom
    gas = gas_velocity
    for sweep in range(SWEEPS):
        gas = (known + VISCOSITY * (jnp.roll(gas, 1, axis=1) + jnp.roll(gas, -1, axis=1))) / diag[None]
    particle_gas = gas[:, index]
    positions_out = pos.transpose(1, 0, 2, 3).reshape(3, -1)
    velocities_out = vel.transpose(1, 0, 2, 3).reshape(3, -1)
    return (positions_out, velocities_out, gas, void_out, particle_gas)
```

```python
import functools

import jax
import jax.numpy as jnp
from jax import lax
from jax.experimental import pallas as pl
from jax.experimental.pallas import tpu as pltpu
from jax.sharding import PartitionSpec as P

NB = 32
BP = 128
NG = 2
NEXT = NB + 2 * NG
NPAIR = 128
GROUP = 8
SUBSTEPS = 4
SWEEPS = 4
K = 5
CHUNKS = 4
DEPROWS = 24
GASROWS = 12

SLAB = 4.0
SOFT = 0.01
STIFF = 20.0
STEP = 0.01
GRAVITY_Z = -1.0
RADIUS_FACTOR = 0.62
CELL_VOLUME = 16.0
RHO_STEP = 2.0
VISCOSITY = 1.0
TINY = 1e-36

F32 = jnp.float32
BF16 = jnp.bfloat16
VMEM = pl.BlockSpec(memory_space=pltpu.VMEM)
SMEM = pl.BlockSpec(memory_space=pltpu.SMEM)
PARAMS = pltpu.CompilerParams(vmem_limit_bytes=40 * 1024 * 1024)


def cost(flops, nbytes, transcendentals=0):
    return pl.CostEstimate(flops=flops, bytes_accessed=nbytes, transcendentals=transcendentals)


def parts3(value):
    high = value.astype(BF16).astype(F32)
    rest = value - high
    mid = rest.astype(BF16).astype(F32)
    low = (rest - mid).astype(BF16).astype(F32)
    return high, mid, low


def swap3(tile):
    return jnp.concatenate([tile[:, 3:6], tile[:, 0:3], tile[:, 6:8]], axis=1)


def fill_sends(par_ref, ghost_ref, state_ref, near_ref, far_ref):
    par = par_ref[0]
    for s in range(NG):
        near_ref[s] = state_ref[ghost_ref[par, s]]
        far_ref[s] = state_ref[ghost_ref[1 - par, s]]


def prepare_kernel(par_ref, ghost_ref, pos_ref, vel_ref, gas_ref, mass_ref, beta_ref, state_ref, aux_ref, near_ref, far_ref):
    radius = RADIUS_FACTOR * jnp.exp(jnp.log(mass_ref[...]) * (1.0 / 3.0))
    zero3 = jnp.zeros((3, BP), F32)
    for b in range(NB):
        lanes = slice(b * BP, (b + 1) * BP)
        rows = slice(b, b + 1)
        state_ref[b] = jnp.concatenate(
            [pos_ref[:, lanes], vel_ref[:, lanes], radius[rows], jnp.zeros((1, BP), F32)], axis=0
        )
        aux_ref[b] = jnp.concatenate([zero3, gas_ref[:, lanes], beta_ref[rows], mass_ref[rows]], axis=0)
    fill_sends(par_ref, ghost_ref, state_ref, near_ref, far_ref)


def prepare(par, ghost_list, pos, vel, gas_seen, mass, beta):
    tile = jax.ShapeDtypeStruct((NB, 8, BP), F32)
    send = jax.ShapeDtypeStruct((NG, 8, BP), F32)
    return pl.pallas_call(
        prepare_kernel,
        in_specs=[SMEM] * 2 + [VMEM] * 5,
        out_shape=(tile, tile, send, send),
        out_specs=(VMEM,) * 4,
        compiler_params=PARAMS,
        cost_estimate=cost(100000, 600000),
        name="prepare",
    )(par, ghost_list, pos, vel, gas_seen, mass, beta)


def pair_body(a, b, ext_ref, jt_ref, g_ref, a_ref, rb_ref):
    both = jnp.dot(jt_ref[b], g_ref[a], preferred_element_type=F32)
    dist2 = both[:, :BP]
    slide = both[:, BP:]
    inv = lax.rsqrt(dist2)
    overlap = (rb_ref[b] + ext_ref[a, 6:7, :]) - dist2 * inv
    delta = jnp.maximum(overlap, 0.0)
    root = delta * lax.rsqrt(jnp.maximum(overlap, TINY))
    push = (root * inv) * (delta - slide * inv)
    push_high = push.astype(BF16)
    push_low = (push - push_high.astype(F32)).astype(BF16)
    root_high = root.astype(BF16)
    root_low = (root - root_high.astype(F32)).astype(BF16)
    weights = jnp.concatenate([push_high, push_low, root_high, root_low], axis=0)
    left_x = a_ref[b, :, :BP]
    left_v = a_ref[b, :, BP:]
    left = jnp.concatenate([left_x, left_x, left_v, left_v], axis=1)
    sums = jnp.dot(left, weights, preferred_element_type=F32)
    return sums[0:8] + sums[8:16] + sums[16:24]


def step_kernel(last, *refs):
    (par_ref, ghost_ref, first_ref, second_ref, owner_ref, cell_ref, state_ref, near_in, far_in, aux_ref), refs = refs[:10], refs[10:]
    if last:
        (pos_out, vel_out, dep_ref), scratch = refs[:3], refs[3:]
    else:
        (new_ref, near_out, far_out), scratch = refs[:3], refs[3:]
    ext_ref, jt_ref, g_ref, a_ref, rb_ref, acc_ref = scratch
    par = par_ref[0]
    row = lax.broadcasted_iota(jnp.int32, (8, BP), 0)[None]

    ext_ref[0:NB] = state_ref[...]
    sign = 1.0 - 2.0 * par.astype(F32)
    shift = jnp.where(row[0] == 0, SLAB * sign, 0.0)
    for s in range(NG):
        ext_ref[NB + NG * (1 - par) + s] = near_in[s] + shift
        ext_ref[NB + NG * par + s] = far_in[s] - shift
    for s in range(NEXT, ext_ref.shape[0]):
        ext_ref[s] = jnp.zeros((8, BP), F32)

    radius = jnp.transpose(ext_ref[:, 6, :])
    for b in range(NEXT):
        rb_ref[b] = jnp.broadcast_to(radius[:, b : b + 1], (BP, BP))

    def features(start, count):
        tile = ext_ref[pl.ds(start, count)]
        swapped = swap3(tile)
        norm = jnp.sum(jnp.where(row < 3, tile * tile, 0.0), axis=1, keepdims=True)
        cross = jnp.sum(jnp.where(row < 3, tile * swapped, 0.0), axis=1, keepdims=True) * (1.0 / STIFF)
        return tile, swapped, norm, cross

    ones = jnp.ones((8, BP), F32)
    zeros = jnp.zeros((8, BP), F32)

    def partner_side(k, carry):
        base = k * 4
        tile, swapped, norm, cross = features(base, 4)
        full = jnp.where(row < 6, tile, jnp.where(row == 6, norm, cross))
        high, mid, low = parts3(full)
        for s in range(4):
            h, m, l = high[s], mid[s], low[s]
            stack = jnp.concatenate([h, h, h, m, m, l, ones, zeros], axis=0)
            jt_ref[base + s] = jnp.transpose(stack).astype(BF16)
            r = row[0]
            by_x = jnp.concatenate(
                [
                    jnp.where(r < 3, h, jnp.where(r == 6, 1.0, 0.0)),
                    jnp.where(r < 3, m, 0.0),
                    jnp.where(r < 3, l, 0.0),
                    zeros,
                ],
                axis=0,
            )
            is_v = (r >= 3) & (r < 6)
            by_v = jnp.concatenate(
                [
                    jnp.where(is_v, h, jnp.where(r == 7, 1.0, 0.0)),
                    jnp.where(is_v, m, 0.0),
                    jnp.where(is_v, l, 0.0),
                    zeros,
                ],
                axis=0,
            )
            a_ref[base + s] = jnp.concatenate([by_x, by_v], axis=1).astype(BF16)
        return carry

    lax.fori_loop(0, NEXT // 4, partner_side, 0)

    def own_side(k, carry):
        base = k * 4
        tile, swapped, norm, cross = features(base, 4)
        xh, xm, xl = parts3(jnp.where(row < 3, -2.0 * tile, 0.0))
        xh = jnp.where(row == 6, 1.0, xh)
        vh, vm, vl = parts3(jnp.where(row < 6, swapped * (-1.0 / STIFF), 0.0))
        vh = jnp.where(row == 7, 1.0, vh)
        nh, nm, nl = parts3(norm + SOFT)
        ch, cm, cl = parts3(cross)
        own_n = jnp.where(row == 0, nh, jnp.where(row == 1, nm, jnp.where(row == 2, nl, 0.0)))
        own_c = jnp.where(row == 0, ch, jnp.where(row == 1, cm, jnp.where(row == 2, cl, 0.0)))
        for s in range(4):
            left = jnp.concatenate([xh[s], xm[s], xl[s], xh[s], xm[s], xh[s], own_n[s], zeros], axis=0)
            right = jnp.concatenate([vh[s], vm[s], vl[s], vh[s], vm[s], vh[s], own_c[s], zeros], axis=0)
            g_ref[base + s] = jnp.concatenate([left, right], axis=1).astype(BF16)
        return carry

    lax.fori_loop(0, NB // 4, own_side, 0)

    acc_ref[...] = jnp.zeros(acc_ref.shape, F32)

    def group(k, carry):
        start = k * GROUP
        firsts = [first_ref[start + s] for s in range(GROUP)]
        seconds = [second_ref[start + s] for s in range(GROUP)]
        sums = [pair_body(a, b, ext_ref, jt_ref, g_ref, a_ref, rb_ref) for a, b in zip(firsts, seconds)]
        for a, value in zip(firsts, sums):
            acc_ref[a] += value
        return carry

    lax.fori_loop(0, NPAIR // GROUP, group, 0)

    tile = state_ref[...]
    acc = acc_ref[...]
    aux = aux_ref[...]
    by_x = STIFF * (tile * acc[:, 6:7] - acc)
    by_v = acc - tile * acc[:, 7:8]
    force = swap3(by_x) + by_v
    beta = aux[:, 6:7]
    mass = aux[:, 7:8]
    gravity = jnp.where(row == 5, GRAVITY_Z, 0.0)
    velocity = tile + STEP * ((force + beta * (aux - tile)) / mass + gravity)
    place = tile + STEP * swap3(velocity)
    moved = jnp.where(row < 3, place, jnp.where(row < 6, velocity, tile))

    if not last:
        new_ref[...] = moved
        fill_sends(par_ref, ghost_ref, new_ref, near_out, far_out)
        return

    for b in range(NB):
        lanes = slice(b * BP, (b + 1) * BP)
        pos_out[:, lanes] = moved[b, 0:3]
        vel_out[:, lanes] = moved[b, 3:6]

    dep_ref[...] = jnp.zeros(dep_ref.shape, F32)
    drag = beta * moved
    quarter = lax.broadcasted_iota(jnp.int32, (DEPROWS, BP), 0) % CHUNKS
    place_of = lax.broadcasted_iota(jnp.int32, (BP, BP), 0)
    tail = jnp.zeros((DEPROWS - CHUNKS * K, BP), F32)
    for b in range(NB):
        cell = cell_ref[b : b + 1, :]
        chunk = cell // BP
        hot = jnp.where(place_of == cell % BP, 1.0, 0.0).astype(BF16)
        values = [mass[b], beta[b], drag[b, 3:4], drag[b, 4:5], drag[b, 5:6]]
        amounts = jnp.concatenate([jnp.broadcast_to(v, (CHUNKS, BP)) for v in values] + [tail], axis=0)
        amounts = jnp.where(quarter == chunk, amounts, 0.0)
        stacked = jnp.concatenate(list(parts3(amounts)) + [zeros], axis=0).astype(BF16)
        spread = lax.dot_general(stacked, hot, (((1,), (1,)), ((), ())), preferred_element_type=F32)
        owner = owner_ref[b]
        dep_ref[owner] += spread[0:DEPROWS] + spread[DEPROWS : 2 * DEPROWS] + spread[2 * DEPROWS : 3 * DEPROWS]


def contact_step(last, ndom, scalars, cells, state, near, far, aux):
    tile = jax.ShapeDtypeStruct((NB, 8, BP), F32)
    send = jax.ShapeDtypeStruct((NG, 8, BP), F32)
    if last:
        flat = jax.ShapeDtypeStruct((3, NB * BP), F32)
        outs = (flat, flat, jax.ShapeDtypeStruct((ndom, DEPROWS, BP), F32))
    else:
        outs = (tile, send, send)
    return pl.pallas_call(
        functools.partial(step_kernel, last),
        in_specs=[SMEM] * 5 + [VMEM] * 5,
        out_shape=outs,
        out_specs=(VMEM,) * 3,
        scratch_shapes=[
            pltpu.VMEM((40, 8, BP), F32),
            pltpu.VMEM((NEXT, BP, 64), BF16),
            pltpu.VMEM((NB, 64, 2 * BP), BF16),
            pltpu.VMEM((NEXT, 32, 2 * BP), BF16),
            pltpu.VMEM((NEXT, BP, BP), F32),
            pltpu.VMEM((NB, 8, BP), F32),
        ],
        compiler_params=PARAMS,
        cost_estimate=cost(1500000000, 2000000, 4000000),
        name="contact_last" if last else "contact",
    )(*scalars, cells, state, near, far, aux)


def known_kernel(dep_ref, gas_ref, void_ref, known_ref, low_ref, high_ref):
    dep = jnp.sum(dep_ref[...], axis=0)
    void = CELL_VOLUME / (CELL_VOLUME + dep[0:4])
    inertia = RHO_STEP * void
    void_ref[...] = void
    rows = [gas_ref[c : c + 1, s * BP : (s + 1) * BP] for c in range(3) for s in range(CHUNKS)]
    gas = [jnp.concatenate(rows[c * CHUNKS : (c + 1) * CHUNKS], axis=0) for c in range(3)]
    diag = inertia + dep[4:8] / CELL_VOLUME + 2.0 * VISCOSITY
    known = [inertia * gas[c] + dep[8 + 4 * c : 12 + 4 * c] / CELL_VOLUME for c in range(3)]
    for s in range(CHUNKS):
        one = slice(s, s + 1)
        tile = jnp.concatenate(
            [g[one] for g in gas] + [k[one] for k in known] + [diag[one], diag[one]], axis=0
        )
        known_ref[s] = tile
    low_ref[...] = known_ref[0]
    high_ref[...] = known_ref[CHUNKS - 1]


def sweeps_kernel(par_ref, near_ref, far_ref, known_ref, gas_out, table_ref):
    odd = par_ref[0] == 1
    below = jnp.where(odd, near_ref[...], far_ref[...])
    above = jnp.where(odd, far_ref[...], near_ref[...])
    full = jnp.concatenate([below] + [known_ref[s] for s in range(CHUNKS)] + [above], axis=1)
    width = full.shape[1]
    inverse = 1.0 / full[6:7]
    known = full[3:6]
    gas = full[0:3]
    pad = jnp.zeros((5, width), F32)
    gas8 = jnp.concatenate([gas, pad], axis=0)
    known8 = jnp.concatenate([known, pad], axis=0)
    for sweep in range(SWEEPS):
        sides = pltpu.roll(gas8, 1, 1) + pltpu.roll(gas8, width - 1, 1)
        gas8 = (known8 + VISCOSITY * sides) * inverse
    gas_out[...] = gas8[0:3, BP : BP + CHUNKS * BP]
    for c in range(3):
        for s in range(CHUNKS):
            table_ref[c * CHUNKS + s : c * CHUNKS + s + 1, :] = gas8[c : c + 1, (s + 1) * BP : (s + 2) * BP]


def pick_kernel(owner_ref, cell_ref, table_ref, out_ref):
    place_of = lax.broadcasted_iota(jnp.int32, (BP, BP), 0)
    quarter = lax.broadcasted_iota(jnp.int32, (CHUNKS, BP), 0)
    pad = jnp.zeros((4, BP), F32)
    for b in range(NB):
        cell = cell_ref[b : b + 1, :]
        chunk = cell // BP
        hot = jnp.where(place_of == cell % BP, 1.0, 0.0).astype(BF16)
        rows = jnp.concatenate([table_ref[owner_ref[b]], pad], axis=0)
        stacked = jnp.concatenate(parts3(rows), axis=0).astype(BF16)
        found = jnp.dot(stacked, hot, preferred_element_type=F32)
        found = found[0:16] + found[16:32] + found[32:48]
        mine = quarter == chunk
        out_ref[:, b * BP : (b + 1) * BP] = jnp.concatenate(
            [
                jnp.sum(jnp.where(mine, found[4 * c : 4 * c + 4], 0.0), axis=0, keepdims=True)
                for c in range(3)
            ],
            axis=0,
        )


def swap_pairs(count):
    near = [(d, d ^ 1) for d in range(count)]
    far = [(d, (d + 1) % count if d % 2 else (d - 1) % count) for d in range(count)]
    return near, far


def body(
    positions,
    velocities,
    particle_volume,
    drag_coef,
    gas_at_particle,
    pair_first,
    pair_second,
    ghost_list,
    block_owner,
    cell_map,
    gas_velocity,
):
    axes = ("grp", "dom")
    ndom = lax.axis_size("dom")
    near_pairs, far_pairs = swap_pairs(lax.axis_size("grp") * ndom)

    def exchange(near, far):
        far = lax.ppermute(far, axes, far_pairs)
        near = lax.ppermute(near, axes, near_pairs)
        return near, far

    par = (lax.axis_index("dom") % 2).astype(jnp.int32).reshape(1)
    mass = particle_volume.reshape(NB, BP)
    beta = drag_coef.reshape(NB, BP)
    cells = cell_map.reshape(NB, BP)
    owner = block_owner.reshape(NB)
    scalars = (par, ghost_list, pair_first, pair_second, owner)

    state, aux, near, far = prepare(par, ghost_list, positions, velocities, gas_at_particle, mass, beta)
    for step in range(SUBSTEPS):
        near, far = exchange(near, far)
        last = step == SUBSTEPS - 1
        state, near, far = contact_step(last, ndom, scalars, cells, state, near, far, aux)
    pos_out, vel_out, dep = state, near, far

    dep = lax.all_to_all(dep, "dom", 0, 0, tiled=True)

    tile = jax.ShapeDtypeStruct((8, BP), F32)
    void, known, low, high = pl.pallas_call(
        known_kernel,
        in_specs=[VMEM] * 2,
        out_shape=(
            jax.ShapeDtypeStruct((CHUNKS, BP), F32),
            jax.ShapeDtypeStruct((CHUNKS, 8, BP), F32),
            tile,
            tile,
        ),
        out_specs=(VMEM,) * 4,
        compiler_params=PARAMS,
        cost_estimate=cost(400000, 1600000),
        name="known",
    )(dep, gas_velocity)
    odd = par[0] == 1
    near, far = exchange(jnp.where(odd, low, high), jnp.where(odd, high, low))
    gas, table = pl.pallas_call(
        sweeps_kernel,
        in_specs=[SMEM] + [VMEM] * 3,
        out_shape=(
            jax.ShapeDtypeStruct((3, CHUNKS * BP), F32),
            jax.ShapeDtypeStruct((GASROWS, BP), F32),
        ),
        out_specs=(VMEM,) * 2,
        compiler_params=PARAMS,
        cost_estimate=cost(40000, 50000),
        name="sweeps",
    )(par, near, far, known)
    table = jnp.broadcast_to(table[None], (ndom, GASROWS, BP))
    table = lax.all_to_all(table, "dom", 0, 0, tiled=True)
    particle_gas = pl.pallas_call(
        pick_kernel,
        in_specs=[SMEM] + [VMEM] * 2,
        out_shape=jax.ShapeDtypeStruct((3, NB * BP), F32),
        out_specs=VMEM,
        compiler_params=PARAMS,
        cost_estimate=cost(60000000, 1200000),
        name="pick",
    )(owner, cells, table)
    return (pos_out, vel_out, gas, void.reshape(-1), particle_gas)


def solution(mesh):
    both = ("grp", "dom")
    return jax.shard_map(
        body,
        mesh=mesh,
        in_specs=(
            P(None, both),
            P(None, both),
            P(both),
            P(both),
            P(None, both),
            P(both),
            P(both),
            P(None, both),
            P(both, None),
            P(both),
            P(None, both),
        ),
        out_specs=(
            P(None, both),
            P(None, both),
            P(None, both),
            P(both),
            P(None, both),
        ),
        check_vma=False,
    )
```

```python
import functools

import jax
import jax.numpy as jnp
from jax import lax
from jax.experimental import pallas as pl
from jax.experimental.pallas import tpu as pltpu
from jax.sharding import PartitionSpec as P

NB = 32
BP = 128
NG = 2
NEXT = NB + 2 * NG
NPAIR = 128
GROUP = 8
SUBSTEPS = 4
SWEEPS = 4
K = 5
CHUNKS = 4
DEPROWS = 24
ROOM = NPAIR + GROUP
LISTS = 4 * ROOM + 8

SLAB = 4.0
SOFT = 0.01
STIFF = 20.0
STEP = 0.01
GRAVITY_Z = -1.0
RADIUS_FACTOR = 0.62
CELL_VOLUME = 16.0
RHO_STEP = 2.0
VISCOSITY = 1.0
TINY = 1e-36

F32 = jnp.float32
BF16 = jnp.bfloat16
VMEM = pl.BlockSpec(memory_space=pltpu.VMEM)
SMEM = pl.BlockSpec(memory_space=pltpu.SMEM)
PARAMS = pltpu.CompilerParams(vmem_limit_bytes=24 * 1024 * 1024)


def cost(flops, nbytes, transcendentals=0):
    return pl.CostEstimate(flops=flops, bytes_accessed=nbytes, transcendentals=transcendentals)


def parts3(value):
    high = value.astype(BF16).astype(F32)
    rest = value - high
    mid = rest.astype(BF16).astype(F32)
    low = (rest - mid).astype(BF16).astype(F32)
    return high, mid, low


def swap3(tile):
    return jnp.concatenate([tile[:, 3:6], tile[:, 0:3], tile[:, 6:8]], axis=1)


def fill_sends(par_ref, ghost_ref, state_ref, near_ref, far_ref):
    par = par_ref[0]
    for s in range(NG):
        near_ref[s] = state_ref[ghost_ref[par, s]]
        far_ref[s] = state_ref[ghost_ref[1 - par, s]]


def prepare_kernel(
    par_ref, ghost_hbm, pos_hbm, vel_hbm, gas_hbm, mass_hbm, beta_hbm, first_hbm, second_hbm,
    state_ref, aux_ref, rb_ref, near_ref, far_ref, list_ref,
    ghost_ref, pos_ref, vel_ref, gas_ref, mass_ref, beta_ref, first_ref, second_ref, sems,
):
    sources = (ghost_hbm, pos_hbm, vel_hbm, gas_hbm, mass_hbm, beta_hbm, first_hbm, second_hbm)
    targets = (ghost_ref, pos_ref, vel_ref, gas_ref, mass_ref, beta_ref, first_ref, second_ref)
    copies = [pltpu.make_async_copy(s, t, sems.at[i]) for i, (s, t) in enumerate(zip(sources, targets))]
    for copy in copies:
        copy.start()
    for copy in copies:
        copy.wait()
    radius = RADIUS_FACTOR * jnp.exp(jnp.log(mass_ref[...]) * (1.0 / 3.0))
    zero3 = jnp.zeros((3, BP), F32)
    for b in range(NB):
        lanes = slice(b * BP, (b + 1) * BP)
        rows = slice(b, b + 1)
        state_ref[b] = jnp.concatenate(
            [pos_ref[:, lanes], vel_ref[:, lanes], radius[rows], jnp.zeros((1, BP), F32)], axis=0
        )
        aux_ref[b] = jnp.concatenate([zero3, gas_ref[:, lanes], beta_ref[rows], mass_ref[rows]], axis=0)
    fill_sends(par_ref, ghost_ref, state_ref, near_ref, far_ref)
    column = jnp.transpose(radius)
    for b in range(NB):
        rb_ref[b] = jnp.broadcast_to(column[:, b : b + 1], (BP, BP))

    def sort_pair(p, counts):
        local, ghost = counts
        first = first_ref[p]
        second = second_ref[p]
        is_ghost = (second >= NB).astype(jnp.int32)
        slot = jnp.where(is_ghost == 1, 2 * ROOM + ghost, local)
        list_ref[slot] = first
        list_ref[ROOM + slot] = second
        return local + 1 - is_ghost, ghost + is_ghost

    local, ghost = lax.fori_loop(0, NPAIR, sort_pair, (jnp.int32(0), jnp.int32(0)))
    for s in range(GROUP):
        list_ref[local + s] = NB
        list_ref[ROOM + local + s] = 0
        list_ref[2 * ROOM + ghost + s] = NB
        list_ref[3 * ROOM + ghost + s] = NB
    list_ref[4 * ROOM] = (local + GROUP - 1) // GROUP
    list_ref[4 * ROOM + 1] = (ghost + GROUP - 1) // GROUP


def prepare(par, ghost_list, pos, vel, gas_seen, mass, beta, first, second):
    tile = jax.ShapeDtypeStruct((NB, 8, BP), F32)
    send = jax.ShapeDtypeStruct((NG, 8, BP), F32)
    wide = jax.ShapeDtypeStruct((NB, BP, BP), F32)
    lists = jax.ShapeDtypeStruct((LISTS,), jnp.int32)
    return pl.pallas_call(
        prepare_kernel,
        in_specs=[SMEM] + [pl.BlockSpec(memory_space=pl.ANY)] * 8,
        out_shape=(tile, tile, wide, send, send, lists),
        out_specs=(VMEM,) * 5 + (SMEM,),
        scratch_shapes=[
            pltpu.SMEM((2, NG), jnp.int32),
            pltpu.VMEM((3, NB * BP), F32),
            pltpu.VMEM((3, NB * BP), F32),
            pltpu.VMEM((3, NB * BP), F32),
            pltpu.VMEM((NB, BP), F32),
            pltpu.VMEM((NB, BP), F32),
            pltpu.SMEM((NPAIR,), jnp.int32),
            pltpu.SMEM((NPAIR,), jnp.int32),
            pltpu.SemaphoreType.DMA((8,)),
        ],
        compiler_params=pltpu.CompilerParams(vmem_limit_bytes=58 * 1024 * 1024),
        cost_estimate=cost(100000, 3000000),
        name="prepare",
    )(par, ghost_list, pos, vel, gas_seen, mass, beta, first, second)


def row_index():
    return lax.broadcasted_iota(jnp.int32, (8, BP), 0)[None]


def features(tile):
    row = row_index()
    swapped = swap3(tile)
    norm = jnp.sum(jnp.where(row < 3, tile * tile, 0.0), axis=1, keepdims=True)
    cross = jnp.sum(jnp.where(row < 3, tile * swapped, 0.0), axis=1, keepdims=True) * (1.0 / STIFF)
    return swapped, norm, cross


def partner_side(tile, base, jt_ref, a_ref):
    row = row_index()
    r = row[0]
    ones = jnp.ones((8, BP), F32)
    zeros = jnp.zeros((8, BP), F32)
    swapped, norm, cross = features(tile)
    full = jnp.where(row < 6, tile, jnp.where(row == 6, norm, cross))
    high, mid, low = parts3(full)
    is_v = (r >= 3) & (r < 6)
    for s in range(4):
        h, m, l = high[s], mid[s], low[s]
        stack = jnp.concatenate([h, h, h, m, m, l, ones, zeros], axis=0)
        jt_ref[base + s] = jnp.transpose(stack).astype(BF16)
        by_x = jnp.concatenate(
            [
                jnp.where(r < 3, h, jnp.where(r == 6, 1.0, 0.0)),
                jnp.where(r < 3, m, 0.0),
                jnp.where(r < 3, l, 0.0),
                zeros,
            ],
            axis=0,
        )
        by_v = jnp.concatenate(
            [
                jnp.where(is_v, h, jnp.where(r == 7, 1.0, 0.0)),
                jnp.where(is_v, m, 0.0),
                jnp.where(is_v, l, 0.0),
                zeros,
            ],
            axis=0,
        )
        a_ref[base + s] = jnp.concatenate([by_x, by_v], axis=1).astype(BF16)


def own_side(tile, base, g_ref):
    row = row_index()
    zeros = jnp.zeros((8, BP), F32)
    swapped, norm, cross = features(tile)
    xh, xm, xl = parts3(jnp.where(row < 3, -2.0 * tile, 0.0))
    xh = jnp.where(row == 6, 1.0, xh)
    vh, vm, vl = parts3(jnp.where(row < 6, swapped * (-1.0 / STIFF), 0.0))
    vh = jnp.where(row == 7, 1.0, vh)
    nh, nm, nl = parts3(norm + SOFT)
    ch, cm, cl = parts3(cross)
    own_n = jnp.where(row == 0, nh, jnp.where(row == 1, nm, jnp.where(row == 2, nl, 0.0)))
    own_c = jnp.where(row == 0, ch, jnp.where(row == 1, cm, jnp.where(row == 2, cl, 0.0)))
    for s in range(4):
        left = jnp.concatenate([xh[s], xm[s], xl[s], xh[s], xm[s], xh[s], own_n[s], zeros], axis=0)
        right = jnp.concatenate([vh[s], vm[s], vl[s], vh[s], vm[s], vh[s], own_c[s], zeros], axis=0)
        g_ref[base + s] = jnp.concatenate([left, right], axis=1).astype(BF16)


def pair_sums(a, b, state_ref, jt_ref, g_ref, a_ref, rb_ref):
    both = jnp.dot(jt_ref[b], g_ref[a], preferred_element_type=F32)
    dist2 = both[:, :BP]
    slide = both[:, BP:]
    inv = lax.rsqrt(dist2)
    overlap = (rb_ref[b] + state_ref[a, 6:7, :]) - dist2 * inv
    delta = jnp.maximum(overlap, 0.0)
    root = delta * lax.rsqrt(jnp.maximum(overlap, TINY))
    push = (root * inv) * (delta - slide * inv)
    push_high = push.astype(BF16)
    push_low = (push - push_high.astype(F32)).astype(BF16)
    root_high = root.astype(BF16)
    root_low = (root - root_high.astype(F32)).astype(BF16)
    weights = jnp.concatenate([push_high, push_low, root_high, root_low], axis=0)
    left_x = a_ref[b, :, :BP]
    left_v = a_ref[b, :, BP:]
    left = jnp.concatenate([left_x, left_x, left_v, left_v], axis=1)
    sums = jnp.dot(left, weights, preferred_element_type=F32)
    return sums[0:8] + sums[8:16] + sums[16:24]


def all_pairs(groups, offset, partner_base, list_ref, acc_ref, state_ref, jt_ref, g_ref, a_ref, rb_ref):
    def group(k, carry):
        start = offset + k * GROUP
        firsts = [list_ref[start + s] for s in range(GROUP)]
        seconds = [list_ref[start + ROOM + s] - partner_base for s in range(GROUP)]
        sums = [
            pair_sums(jnp.minimum(a, NB - 1), b, state_ref, jt_ref, g_ref, a_ref, rb_ref)
            for a, b in zip(firsts, seconds)
        ]
        for a, value in zip(firsts, sums):
            acc_ref[a] += value
        return carry

    lax.fori_loop(0, groups, group, 0)


def local_kernel(list_ref, state_ref, rb_ref, acc_ref, g_ref, jt_ref, a_ref):
    def blocks(k, carry):
        tile = state_ref[pl.ds(k * 4, 4)]
        partner_side(tile, k * 4, jt_ref, a_ref)
        own_side(tile, k * 4, g_ref)
        return carry

    lax.fori_loop(0, NB // 4, blocks, 0)
    acc_ref[...] = jnp.zeros(acc_ref.shape, F32)
    all_pairs(list_ref[4 * ROOM], 0, 0, list_ref, acc_ref, state_ref, jt_ref, g_ref, a_ref, rb_ref)


def local_pairs(lists, state, rb):
    return pl.pallas_call(
        local_kernel,
        in_specs=[SMEM] + [VMEM] * 2,
        out_shape=(
            jax.ShapeDtypeStruct((NB + 1, 8, BP), F32),
            jax.ShapeDtypeStruct((NB, 64, 2 * BP), BF16),
        ),
        out_specs=(VMEM,) * 2,
        scratch_shapes=[pltpu.VMEM((NB, BP, 64), BF16), pltpu.VMEM((NB, 32, 2 * BP), BF16)],
        compiler_params=PARAMS,
        cost_estimate=cost(10000000000, 3500000, 4000000),
        name="local_pairs",
    )(lists, state, rb)


def ghost_kernel(last, *refs):
    (par_ref, ghost_ref, list_ref, owner_ref), refs = refs[:4], refs[4:]
    (cell_ref, state_ref, near_in, far_in, aux_ref, part_ref, g_ref), refs = refs[:7], refs[7:]
    if last:
        (pos_out, vel_out, keep_ref, give_ref), scratch = refs[:4], refs[4:]
    else:
        (new_ref, near_out, far_out), scratch = refs[:3], refs[3:]
    ext_ref, jt_ref, a_ref, rb_ref, acc_ref = scratch
    par = par_ref[0]
    row = row_index()

    sign = 1.0 - 2.0 * par.astype(F32)
    shift = jnp.where(row[0] == 0, SLAB * sign, 0.0)
    for s in range(NG):
        ext_ref[NG * (1 - par) + s] = near_in[s] + shift
        ext_ref[NG * par + s] = far_in[s] - shift
    for s in range(2 * NG, 8):
        ext_ref[s] = jnp.zeros((8, BP), F32)
    column = jnp.transpose(ext_ref[:, 6, :])
    for b in range(2 * NG):
        rb_ref[b] = jnp.broadcast_to(column[:, b : b + 1], (BP, BP))
    partner_side(ext_ref[0:4], 0, jt_ref, a_ref)
    acc_ref[...] = part_ref[...]
    all_pairs(
        list_ref[4 * ROOM + 1], 2 * ROOM, NB, list_ref, acc_ref, state_ref, jt_ref, g_ref, a_ref, rb_ref
    )

    tile = state_ref[...]
    acc = acc_ref[0:NB]
    aux = aux_ref[...]
    by_x = STIFF * (tile * acc[:, 6:7] - acc)
    by_v = acc - tile * acc[:, 7:8]
    force = swap3(by_x) + by_v
    beta = aux[:, 6:7]
    mass = aux[:, 7:8]
    gravity = jnp.where(row == 5, GRAVITY_Z, 0.0)
    velocity = tile + STEP * ((force + beta * (aux - tile)) / mass + gravity)
    place = tile + STEP * swap3(velocity)
    moved = jnp.where(row < 3, place, jnp.where(row < 6, velocity, tile))

    if not last:
        new_ref[...] = moved
        fill_sends(par_ref, ghost_ref, new_ref, near_out, far_out)
        return

    for b in range(NB):
        lanes = slice(b * BP, (b + 1) * BP)
        pos_out[:, lanes] = moved[b, 0:3]
        vel_out[:, lanes] = moved[b, 3:6]

    keep_ref[...] = jnp.zeros(keep_ref.shape, F32)
    give_ref[...] = jnp.zeros(give_ref.shape, F32)
    drag = beta * moved
    quarter = lax.broadcasted_iota(jnp.int32, (DEPROWS, BP), 0) % CHUNKS
    place_of = lax.broadcasted_iota(jnp.int32, (BP, BP), 0)
    zeros = jnp.zeros((8, BP), F32)
    tail = jnp.zeros((DEPROWS - CHUNKS * K, BP), F32)
    for b in range(NB):
        cell = cell_ref[b : b + 1, :]
        chunk = cell // BP
        hot = jnp.where(place_of == cell % BP, 1.0, 0.0).astype(BF16)
        values = [mass[b], beta[b], drag[b, 3:4], drag[b, 4:5], drag[b, 5:6]]
        amounts = jnp.concatenate([jnp.broadcast_to(v, (CHUNKS, BP)) for v in values] + [tail], axis=0)
        amounts = jnp.where(quarter == chunk, amounts, 0.0)
        stacked = jnp.concatenate(list(parts3(amounts)) + [zeros], axis=0).astype(BF16)
        spread = lax.dot_general(stacked, hot, (((1,), (1,)), ((), ())), preferred_element_type=F32)
        spread = spread[0:DEPROWS] + spread[DEPROWS : 2 * DEPROWS] + spread[2 * DEPROWS : 3 * DEPROWS]
        owner = owner_ref[b]
        chip = owner // 2
        mine = owner % 2 == par

        def put(target, chip=chip, spread=spread):
            for q in range(K):
                target[chip, q] += spread[CHUNKS * q : CHUNKS * (q + 1)]

        pl.when(mine)(functools.partial(put, keep_ref))
        pl.when(jnp.logical_not(mine))(functools.partial(put, give_ref))


def ghost_pairs(last, chips, scalars, cells, state, near, far, aux, part, g):
    tile = jax.ShapeDtypeStruct((NB, 8, BP), F32)
    send = jax.ShapeDtypeStruct((NG, 8, BP), F32)
    if last:
        flat = jax.ShapeDtypeStruct((3, NB * BP), F32)
        dep = jax.ShapeDtypeStruct((chips, K, CHUNKS, BP), F32)
        outs = (flat, flat, dep, dep)
    else:
        outs = (tile, send, send)
    return pl.pallas_call(
        functools.partial(ghost_kernel, last),
        in_specs=[SMEM] * 4 + [VMEM] * 7,
        out_shape=outs,
        out_specs=(VMEM,) * len(outs),
        scratch_shapes=[
            pltpu.VMEM((8, 8, BP), F32),
            pltpu.VMEM((2 * NG, BP, 64), BF16),
            pltpu.VMEM((2 * NG, 32, 2 * BP), BF16),
            pltpu.VMEM((2 * NG, BP, BP), F32),
            pltpu.VMEM((NB + 1, 8, BP), F32),
        ],
        compiler_params=PARAMS,
        cost_estimate=cost(2000000000, 2000000, 500000),
        name="ghost_pairs_last" if last else "ghost_pairs",
    )(*scalars, cells, state, near, far, aux, part, g)


def known_kernel(dep_ref, gas_ref, void_ref, known_ref, low_ref, high_ref):
    dep = jnp.sum(dep_ref[...], axis=0)
    void = CELL_VOLUME / (CELL_VOLUME + dep[0])
    inertia = RHO_STEP * void
    void_ref[...] = void
    gas = [
        jnp.concatenate([gas_ref[c : c + 1, s * BP : (s + 1) * BP] for s in range(CHUNKS)], axis=0)
        for c in range(3)
    ]
    diag = inertia + dep[1] / CELL_VOLUME + 2.0 * VISCOSITY
    known = [inertia * gas[c] + dep[2 + c] / CELL_VOLUME for c in range(3)]
    for s in range(CHUNKS):
        one = slice(s, s + 1)
        known_ref[s] = jnp.concatenate(
            [g[one] for g in gas] + [k[one] for k in known] + [diag[one], diag[one]], axis=0
        )
    low_ref[...] = known_ref[0]
    high_ref[...] = known_ref[CHUNKS - 1]


def sweeps_kernel(par_ref, near_ref, far_ref, known_ref, gas_out, table_ref):
    odd = par_ref[0] == 1
    below = jnp.where(odd, near_ref[...], far_ref[...])
    above = jnp.where(odd, far_ref[...], near_ref[...])
    full = jnp.concatenate([below] + [known_ref[s] for s in range(CHUNKS)] + [above], axis=1)
    width = full.shape[1]
    inverse = 1.0 / full[6:7]
    pad = jnp.zeros((5, width), F32)
    gas = jnp.concatenate([full[0:3], pad], axis=0)
    known = jnp.concatenate([full[3:6], pad], axis=0)
    for sweep in range(SWEEPS):
        sides = pltpu.roll(gas, 1, 1) + pltpu.roll(gas, width - 1, 1)
        gas = (known + VISCOSITY * sides) * inverse
    gas_out[...] = gas[0:3, BP : BP + CHUNKS * BP]
    for c in range(3):
        for s in range(CHUNKS):
            table_ref[c, s : s + 1, :] = gas[c : c + 1, (s + 1) * BP : (s + 2) * BP]


def pick_kernel(par_ref, owner_ref, cell_ref, mine_ref, other_ref, out_ref):
    par = par_ref[0]
    place_of = lax.broadcasted_iota(jnp.int32, (BP, BP), 0)
    quarter = lax.broadcasted_iota(jnp.int32, (CHUNKS, BP), 0)
    pad = jnp.zeros((4, BP), F32)
    for b in range(NB):
        cell = cell_ref[b : b + 1, :]
        chunk = cell // BP
        hot = jnp.where(place_of == cell % BP, 1.0, 0.0).astype(BF16)
        owner = owner_ref[b]
        chip = owner // 2
        mine = owner % 2 == par
        rows = [jnp.where(mine, mine_ref[chip, c], other_ref[chip, c]) for c in range(3)]
        rows = jnp.concatenate(rows + [pad], axis=0)
        stacked = jnp.concatenate(parts3(rows), axis=0).astype(BF16)
        found = jnp.dot(stacked, hot, preferred_element_type=F32)
        found = found[0:16] + found[16:32] + found[32:48]
        here = quarter == chunk
        out_ref[:, b * BP : (b + 1) * BP] = jnp.concatenate(
            [
                jnp.sum(jnp.where(here, found[4 * c : 4 * c + 4], 0.0), axis=0, keepdims=True)
                for c in range(3)
            ],
            axis=0,
        )


def swap_pairs(count):
    near = [(d, d ^ 1) for d in range(count)]
    far = [(d, (d + 1) % count if d % 2 else (d - 1) % count) for d in range(count)]
    return near, far


def body(
    positions,
    velocities,
    particle_volume,
    drag_coef,
    gas_at_particle,
    pair_first,
    pair_second,
    ghost_list,
    block_owner,
    cell_map,
    gas_velocity,
):
    axes = ("grp", "dom")
    ndom = lax.axis_size("dom")
    near_pairs, far_pairs = swap_pairs(lax.axis_size("grp") * ndom)

    def exchange(near, far):
        far = lax.ppermute(far, axes, far_pairs)
        near = lax.ppermute(near, axes, near_pairs)
        return near, far

    par = (lax.axis_index("dom") & 1).astype(jnp.int32).reshape(1)
    chips = ndom // 2
    same_core = [list(range(core, ndom, 2)) for core in range(2)]
    mass = particle_volume.reshape(NB, BP)
    beta = drag_coef.reshape(NB, BP)
    cells = cell_map.reshape(NB, BP)
    owner = block_owner.reshape(NB)

    state, aux, rb, near, far, lists = prepare(
        par, ghost_list, positions, velocities, gas_at_particle, mass, beta, pair_first, pair_second
    )
    scalars = (par, ghost_list, lists, owner)
    for step in range(SUBSTEPS):
        near, far = exchange(near, far)
        part, g = local_pairs(lists, state, rb)
        last = step == SUBSTEPS - 1
        outs = ghost_pairs(last, chips, scalars, cells, state, near, far, aux, part, g)
        if not last:
            state, near, far = outs
    pos_out, vel_out, keep, give = outs

    dep = keep + lax.ppermute(give, axes, near_pairs)
    dep = lax.all_to_all(dep, "dom", 0, 0, axis_index_groups=same_core, tiled=True)

    tile = jax.ShapeDtypeStruct((8, BP), F32)
    void, known, low, high = pl.pallas_call(
        known_kernel,
        in_specs=[VMEM] * 2,
        out_shape=(
            jax.ShapeDtypeStruct((CHUNKS, BP), F32),
            jax.ShapeDtypeStruct((CHUNKS, 8, BP), F32),
            tile,
            tile,
        ),
        out_specs=(VMEM,) * 4,
        compiler_params=PARAMS,
        cost_estimate=cost(400000, 700000),
        name="known",
    )(dep, gas_velocity)
    odd = par[0] == 1
    near, far = exchange(jnp.where(odd, low, high), jnp.where(odd, high, low))
    gas, table = pl.pallas_call(
        sweeps_kernel,
        in_specs=[SMEM] + [VMEM] * 3,
        out_shape=(
            jax.ShapeDtypeStruct((3, CHUNKS * BP), F32),
            jax.ShapeDtypeStruct((3, CHUNKS, BP), F32),
        ),
        out_specs=(VMEM,) * 2,
        compiler_params=PARAMS,
        cost_estimate=cost(40000, 50000),
        name="sweeps",
    )(par, near, far, known)

    table = jnp.broadcast_to(table[None], (chips, 3, CHUNKS, BP))
    table = lax.all_to_all(table, "dom", 0, 0, axis_index_groups=same_core, tiled=True)
    other = lax.ppermute(table, axes, near_pairs)
    particle_gas = pl.pallas_call(
        pick_kernel,
        in_specs=[SMEM] * 2 + [VMEM] * 3,
        out_shape=jax.ShapeDtypeStruct((3, NB * BP), F32),
        out_specs=VMEM,
        compiler_params=PARAMS,
        cost_estimate=cost(60000000, 900000),
        name="pick",
    )(par, owner, cells, table, other)
    return (pos_out, vel_out, gas, void.reshape(-1), particle_gas)


def solution(mesh):
    both = ("grp", "dom")
    return jax.shard_map(
        body,
        mesh=mesh,
        in_specs=(
            P(None, both),
            P(None, both),
            P(both),
            P(both),
            P(None, both),
            P(both),
            P(both),
            P(None, both),
            P(both, None),
            P(both),
            P(None, both),
        ),
        out_specs=(
            P(None, both),
            P(None, both),
            P(None, both),
            P(both),
            P(None, both),
        ),
        check_vma=False,
    )
```

```python
import functools

import jax
import jax.numpy as jnp
from jax import lax
from jax.experimental import pallas as pl
from jax.experimental.pallas import tpu as pltpu
from jax.sharding import PartitionSpec as P

NB = 32
BP = 128
NG = 2
NEXT = NB + 2 * NG
NPAIR = 128
GROUP = 8
SUBSTEPS = 4
SWEEPS = 4
K = 5
CHUNKS = 4
DEPROWS = 24
ROOM = NPAIR + 2 * GROUP
LISTS = 4 * ROOM + 8

SLAB = 4.0
SOFT = 0.01
STIFF = 20.0
STEP = 0.01
GRAVITY_Z = -1.0
RADIUS_FACTOR = 0.62
CELL_VOLUME = 16.0
RHO_STEP = 2.0
VISCOSITY = 1.0
TINY = 1e-36

F32 = jnp.float32
BF16 = jnp.bfloat16
VMEM = pl.BlockSpec(memory_space=pltpu.VMEM)
SMEM = pl.BlockSpec(memory_space=pltpu.SMEM)
PARAMS = pltpu.CompilerParams(vmem_limit_bytes=24 * 1024 * 1024)


def cost(flops, nbytes, transcendentals=0):
    return pl.CostEstimate(flops=flops, bytes_accessed=nbytes, transcendentals=transcendentals)


def parts3(value):
    high = value.astype(BF16).astype(F32)
    rest = value - high
    mid = rest.astype(BF16).astype(F32)
    low = (rest - mid).astype(BF16).astype(F32)
    return high, mid, low


def swap3(tile):
    return jnp.concatenate([tile[:, 3:6], tile[:, 0:3], tile[:, 6:8]], axis=1)


def fill_sends(par_ref, ghost_ref, state_ref, near_ref, far_ref):
    par = par_ref[0]
    for s in range(NG):
        near_ref[s] = state_ref[ghost_ref[par, s]]
        far_ref[s] = state_ref[ghost_ref[1 - par, s]]


def prepare_kernel(
    par_ref, ghost_hbm, pos_hbm, vel_hbm, gas_hbm, mass_hbm, beta_hbm, first_hbm, second_hbm,
    state_ref, aux_ref, near_ref, far_ref, list_ref,
    ghost_ref, pos_ref, vel_ref, gas_ref, mass_ref, beta_ref, first_ref, second_ref, sems,
):
    sources = (ghost_hbm, pos_hbm, vel_hbm, gas_hbm, mass_hbm, beta_hbm, first_hbm, second_hbm)
    targets = (ghost_ref, pos_ref, vel_ref, gas_ref, mass_ref, beta_ref, first_ref, second_ref)
    copies = [pltpu.make_async_copy(s, t, sems.at[i]) for i, (s, t) in enumerate(zip(sources, targets))]
    for copy in copies:
        copy.start()
    for copy in copies:
        copy.wait()
    radius = RADIUS_FACTOR * jnp.exp(jnp.log(mass_ref[...]) * (1.0 / 3.0))
    zero3 = jnp.zeros((3, BP), F32)
    for b in range(NB):
        lanes = slice(b * BP, (b + 1) * BP)
        rows = slice(b, b + 1)
        state_ref[b] = jnp.concatenate(
            [pos_ref[:, lanes], vel_ref[:, lanes], radius[rows], jnp.zeros((1, BP), F32)], axis=0
        )
        aux_ref[b] = jnp.concatenate([zero3, gas_ref[:, lanes], beta_ref[rows], mass_ref[rows]], axis=0)
    fill_sends(par_ref, ghost_ref, state_ref, near_ref, far_ref)

    def sort_pair(p, counts):
        local, ghost = counts
        first = first_ref[p]
        second = second_ref[p]
        is_ghost = (second >= NB).astype(jnp.int32)
        slot = jnp.where(is_ghost == 1, 2 * ROOM + ghost, GROUP + local)
        list_ref[slot] = first
        list_ref[ROOM + slot] = second
        return local + 1 - is_ghost, ghost + is_ghost

    local, ghost = lax.fori_loop(0, NPAIR, sort_pair, (jnp.int32(0), jnp.int32(0)))
    for s in range(GROUP):
        list_ref[s] = NB
        list_ref[ROOM + s] = 0
        list_ref[GROUP + local + s] = NB
        list_ref[ROOM + GROUP + local + s] = 0
        list_ref[2 * ROOM + ghost + s] = NB
        list_ref[3 * ROOM + ghost + s] = NB
    list_ref[4 * ROOM] = (local + GROUP - 1) // GROUP
    list_ref[4 * ROOM + 1] = (ghost + GROUP - 1) // GROUP


def prepare(par, ghost_list, pos, vel, gas_seen, mass, beta, first, second):
    tile = jax.ShapeDtypeStruct((NB, 8, BP), F32)
    send = jax.ShapeDtypeStruct((NG, 8, BP), F32)
    lists = jax.ShapeDtypeStruct((LISTS,), jnp.int32)
    return pl.pallas_call(
        prepare_kernel,
        in_specs=[SMEM] + [pl.BlockSpec(memory_space=pl.ANY)] * 8,
        out_shape=(tile, tile, send, send, lists),
        out_specs=(VMEM,) * 4 + (SMEM,),
        scratch_shapes=[
            pltpu.SMEM((2, NG), jnp.int32),
            pltpu.VMEM((3, NB * BP), F32),
            pltpu.VMEM((3, NB * BP), F32),
            pltpu.VMEM((3, NB * BP), F32),
            pltpu.VMEM((NB, BP), F32),
            pltpu.VMEM((NB, BP), F32),
            pltpu.SMEM((NPAIR,), jnp.int32),
            pltpu.SMEM((NPAIR,), jnp.int32),
            pltpu.SemaphoreType.DMA((8,)),
        ],
        compiler_params=pltpu.CompilerParams(vmem_limit_bytes=58 * 1024 * 1024),
        cost_estimate=cost(100000, 600000),
        name="prepare",
    )(par, ghost_list, pos, vel, gas_seen, mass, beta, first, second)


def row_index():
    return lax.broadcasted_iota(jnp.int32, (8, BP), 0)[None]


def features(tile):
    row = row_index()
    swapped = swap3(tile)
    norm = jnp.sum(jnp.where(row < 3, tile * tile, 0.0), axis=1, keepdims=True)
    cross = jnp.sum(jnp.where(row < 3, tile * swapped, 0.0), axis=1, keepdims=True) * (1.0 / STIFF)
    return swapped, norm, cross


def partner_side(tile, base, jt_ref, a_ref):
    row = row_index()
    r = row[0]
    ones = jnp.ones((8, BP), F32)
    zeros = jnp.zeros((8, BP), F32)
    swapped, norm, cross = features(tile)
    full = jnp.where(row < 6, tile, jnp.where(row == 6, norm, cross))
    high, mid, low = parts3(full)
    is_v = (r >= 3) & (r < 6)
    for s in range(4):
        h, m, l = high[s], mid[s], low[s]
        stack = jnp.concatenate([h, h, h, m, m, l, ones, zeros], axis=0)
        jt_ref[base + s] = jnp.transpose(stack).astype(BF16)
        by_x = jnp.concatenate(
            [
                jnp.where(r < 3, h, jnp.where(r == 6, 1.0, 0.0)),
                jnp.where(r < 3, m, 0.0),
                jnp.where(r < 3, l, 0.0),
                zeros,
            ],
            axis=0,
        )
        by_v = jnp.concatenate(
            [
                jnp.where(is_v, h, jnp.where(r == 7, 1.0, 0.0)),
                jnp.where(is_v, m, 0.0),
                jnp.where(is_v, l, 0.0),
                zeros,
            ],
            axis=0,
        )
        a_ref[base + s] = jnp.concatenate([by_x, by_v], axis=1).astype(BF16)


def own_side(tile, base, g_ref):
    row = row_index()
    zeros = jnp.zeros((8, BP), F32)
    swapped, norm, cross = features(tile)
    xh, xm, xl = parts3(jnp.where(row < 3, -2.0 * tile, 0.0))
    xh = jnp.where(row == 6, 1.0, xh)
    vh, vm, vl = parts3(jnp.where(row < 6, swapped * (-1.0 / STIFF), 0.0))
    vh = jnp.where(row == 7, 1.0, vh)
    nh, nm, nl = parts3(norm + SOFT)
    ch, cm, cl = parts3(cross)
    own_n = jnp.where(row == 0, nh, jnp.where(row == 1, nm, jnp.where(row == 2, nl, 0.0)))
    own_c = jnp.where(row == 0, ch, jnp.where(row == 1, cm, jnp.where(row == 2, cl, 0.0)))
    for s in range(4):
        left = jnp.concatenate([xh[s], xm[s], xl[s], xh[s], xm[s], xh[s], own_n[s], zeros], axis=0)
        right = jnp.concatenate([vh[s], vm[s], vl[s], vh[s], vm[s], vh[s], own_c[s], zeros], axis=0)
        g_ref[base + s] = jnp.concatenate([left, right], axis=1).astype(BF16)


def pair_product(a, b, jt_ref, g_ref):
    return jnp.dot(jt_ref[b], g_ref[a], preferred_element_type=F32)


def pair_weights(both, a, b, state_ref, rb_ref):
    dist2 = both[:, :BP]
    slide = both[:, BP:]
    inv = lax.rsqrt(dist2)
    overlap = (rb_ref[b] + state_ref[a, 6:7, :]) - dist2 * inv
    delta = jnp.maximum(overlap, 0.0)
    root = delta * lax.rsqrt(jnp.maximum(overlap, TINY))
    push = (root * inv) * (delta - slide * inv)
    push_high = push.astype(BF16)
    push_low = (push - push_high.astype(F32)).astype(BF16)
    root_high = root.astype(BF16)
    root_low = (root - root_high.astype(F32)).astype(BF16)
    return jnp.concatenate([push_high, push_low, root_high, root_low], axis=0)


def partner_sums(b, weights, a_ref):
    left_x = a_ref[b, :, :BP]
    left_v = a_ref[b, :, BP:]
    left = jnp.concatenate([left_x, left_x, left_v, left_v], axis=1)
    sums = jnp.dot(left, weights, preferred_element_type=F32)
    return sums[0:8] + sums[8:16] + sums[16:24]


def ghost_loop(groups, list_ref, acc_ref, state_ref, jt_ref, g_ref, a_ref, rb_ref):
    def group(k, carry):
        start = 2 * ROOM + k * GROUP
        firsts = [list_ref[start + s] for s in range(GROUP)]
        sums = []
        for s in range(GROUP):
            a = jnp.minimum(firsts[s], NB - 1)
            b = list_ref[start + ROOM + s] - NB
            weights = pair_weights(pair_product(a, b, jt_ref, g_ref), a, b, state_ref, rb_ref)
            sums.append(partner_sums(b, weights, a_ref))
        for a, value in zip(firsts, sums):
            acc_ref[a] += value
        return carry

    lax.fori_loop(0, groups, group, 0)


def local_loop(groups, list_ref, acc_ref, state_ref, jt_ref, g_ref, a_ref, rb_ref, held_ref):
    def finish(start, s):
        a = list_ref[start + s]
        b = list_ref[ROOM + start + s]
        acc_ref[a] += partner_sums(b, held_ref[s], a_ref)

    def group(k, carry):
        start = k * GROUP
        for s in range(GROUP):
            a = jnp.minimum(list_ref[start + GROUP + s], NB - 1)
            b = list_ref[ROOM + start + GROUP + s]
            both = pair_product(a, b, jt_ref, g_ref)
            finish(start, s)
            held_ref[s] = pair_weights(both, a, b, state_ref, rb_ref)
        return carry

    held_ref[...] = jnp.zeros(held_ref.shape, BF16)
    lax.fori_loop(0, groups, group, 0)
    for s in range(GROUP):
        finish(groups * GROUP, s)


def local_kernel(opening, *refs):
    if opening:
        list_ref, state_ref, acc_ref, g_ref, rb_ref, jt_ref, a_ref, held_ref = refs
        column = jnp.transpose(state_ref[:, 6, :])
        for b in range(NB):
            rb_ref[b] = jnp.broadcast_to(column[:, b : b + 1], (BP, BP))
    else:
        list_ref, state_ref, rb_ref, acc_ref, g_ref, jt_ref, a_ref, held_ref = refs

    def blocks(k, carry):
        tile = state_ref[pl.ds(k * 4, 4)]
        partner_side(tile, k * 4, jt_ref, a_ref)
        own_side(tile, k * 4, g_ref)
        return carry

    lax.fori_loop(0, NB // 4, blocks, 0)
    acc_ref[...] = jnp.zeros(acc_ref.shape, F32)
    local_loop(list_ref[4 * ROOM], list_ref, acc_ref, state_ref, jt_ref, g_ref, a_ref, rb_ref, held_ref)


def local_pairs(lists, state, rb=None):
    opening = rb is None
    outs = (
        jax.ShapeDtypeStruct((NB + 1, 8, BP), F32),
        jax.ShapeDtypeStruct((NB, 64, 2 * BP), BF16),
    )
    wide = (jax.ShapeDtypeStruct((NB, BP, BP), F32),)
    args = (lists, state) if opening else (lists, state, rb)
    outs = pl.pallas_call(
        functools.partial(local_kernel, opening),
        in_specs=[SMEM] + [VMEM] * (len(args) - 1),
        out_shape=outs + (wide if opening else ()),
        out_specs=(VMEM,) * (3 if opening else 2),
        scratch_shapes=[
            pltpu.VMEM((NB, BP, 64), BF16),
            pltpu.VMEM((NB, 32, 2 * BP), BF16),
            pltpu.VMEM((GROUP, 4 * BP, BP), BF16),
        ],
        compiler_params=PARAMS,
        cost_estimate=cost(10000000000, 3500000, 4000000),
        name="local_pairs",
    )(*args)
    return outs if opening else (*outs, rb)


def ghost_kernel(last, *refs):
    (par_ref, ghost_ref, list_ref, owner_ref), refs = refs[:4], refs[4:]
    (cell_ref, state_ref, near_in, far_in, aux_ref, part_ref, g_ref), refs = refs[:7], refs[7:]
    if last:
        (pos_out, vel_out, keep_ref, give_ref), (*scratch, spread_ref) = refs[:4], refs[4:]
    else:
        (new_ref, near_out, far_out), scratch = refs[:3], refs[3:]
    ext_ref, jt_ref, a_ref, rb_ref, acc_ref = scratch
    par = par_ref[0]
    row = row_index()

    sign = 1.0 - 2.0 * par.astype(F32)
    shift = jnp.where(row[0] == 0, SLAB * sign, 0.0)
    for s in range(NG):
        ext_ref[NG * (1 - par) + s] = near_in[s] + shift
        ext_ref[NG * par + s] = far_in[s] - shift
    for s in range(2 * NG, 8):
        ext_ref[s] = jnp.zeros((8, BP), F32)
    column = jnp.transpose(ext_ref[:, 6, :])
    for b in range(2 * NG):
        rb_ref[b] = jnp.broadcast_to(column[:, b : b + 1], (BP, BP))
    partner_side(ext_ref[0:4], 0, jt_ref, a_ref)
    acc_ref[...] = part_ref[...]
    ghost_loop(list_ref[4 * ROOM + 1], list_ref, acc_ref, state_ref, jt_ref, g_ref, a_ref, rb_ref)

    tile = state_ref[...]
    acc = acc_ref[0:NB]
    aux = aux_ref[...]
    by_x = STIFF * (tile * acc[:, 6:7] - acc)
    by_v = acc - tile * acc[:, 7:8]
    force = swap3(by_x) + by_v
    beta = aux[:, 6:7]
    mass = aux[:, 7:8]
    gravity = jnp.where(row == 5, GRAVITY_Z, 0.0)
    velocity = tile + STEP * ((force + beta * (aux - tile)) / mass + gravity)
    place = tile + STEP * swap3(velocity)
    moved = jnp.where(row < 3, place, jnp.where(row < 6, velocity, tile))

    if not last:
        new_ref[...] = moved
        fill_sends(par_ref, ghost_ref, new_ref, near_out, far_out)
        return

    for b in range(NB):
        lanes = slice(b * BP, (b + 1) * BP)
        pos_out[:, lanes] = moved[b, 0:3]
        vel_out[:, lanes] = moved[b, 3:6]

    keep_ref[...] = jnp.zeros(keep_ref.shape, F32)
    give_ref[...] = jnp.zeros(give_ref.shape, F32)
    drag = beta * moved
    quarter = lax.broadcasted_iota(jnp.int32, (DEPROWS, BP), 0) % CHUNKS
    place_of = lax.broadcasted_iota(jnp.int32, (BP, BP), 0)
    zeros = jnp.zeros((8, BP), F32)
    tail = jnp.zeros((DEPROWS - CHUNKS * K, BP), F32)
    for b in range(NB):
        cell = cell_ref[b : b + 1, :]
        chunk = cell // BP
        hot = jnp.where(place_of == cell % BP, 1.0, 0.0).astype(BF16)
        values = [mass[b], beta[b], drag[b, 3:4], drag[b, 4:5], drag[b, 5:6]]
        amounts = jnp.concatenate([jnp.broadcast_to(v, (CHUNKS, BP)) for v in values] + [tail], axis=0)
        amounts = jnp.where(quarter == chunk, amounts, 0.0)
        stacked = jnp.concatenate(list(parts3(amounts)) + [zeros], axis=0).astype(BF16)
        spread = lax.dot_general(stacked, hot, (((1,), (1,)), ((), ())), preferred_element_type=F32)
        spread_ref[b] = spread[0:DEPROWS] + spread[DEPROWS : 2 * DEPROWS] + spread[2 * DEPROWS : 3 * DEPROWS]

    for b in range(NB):
        owner = owner_ref[b]

        def put(target, b=b, chip=owner // 2):
            for q in range(K):
                target[chip, q] += spread_ref[b, CHUNKS * q : CHUNKS * (q + 1)]

        mine = owner % 2 == par
        pl.when(mine)(functools.partial(put, keep_ref))
        pl.when(jnp.logical_not(mine))(functools.partial(put, give_ref))


def ghost_pairs(last, chips, scalars, cells, state, near, far, aux, part, g):
    tile = jax.ShapeDtypeStruct((NB, 8, BP), F32)
    send = jax.ShapeDtypeStruct((NG, 8, BP), F32)
    if last:
        flat = jax.ShapeDtypeStruct((3, NB * BP), F32)
        dep = jax.ShapeDtypeStruct((chips, K, CHUNKS, BP), F32)
        outs = (flat, flat, dep, dep)
    else:
        outs = (tile, send, send)
    return pl.pallas_call(
        functools.partial(ghost_kernel, last),
        in_specs=[SMEM] * 4 + [VMEM] * 7,
        out_shape=outs,
        out_specs=(VMEM,) * len(outs),
        scratch_shapes=[
            pltpu.VMEM((8, 8, BP), F32),
            pltpu.VMEM((2 * NG, BP, 64), BF16),
            pltpu.VMEM((2 * NG, 32, 2 * BP), BF16),
            pltpu.VMEM((2 * NG, BP, BP), F32),
            pltpu.VMEM((NB + 1, 8, BP), F32),
        ]
        + ([pltpu.VMEM((NB, DEPROWS, BP), F32)] if last else []),
        compiler_params=PARAMS,
        cost_estimate=cost(2000000000, 2000000, 500000),
        name="ghost_pairs_last" if last else "ghost_pairs",
    )(*scalars, cells, state, near, far, aux, part, g)


def known_kernel(dep_ref, gas_ref, void_ref, known_ref, low_ref, high_ref):
    dep = jnp.sum(dep_ref[...], axis=0)
    void = CELL_VOLUME / (CELL_VOLUME + dep[0])
    inertia = RHO_STEP * void
    void_ref[...] = void
    gas = [
        jnp.concatenate([gas_ref[c : c + 1, s * BP : (s + 1) * BP] for s in range(CHUNKS)], axis=0)
        for c in range(3)
    ]
    diag = inertia + dep[1] / CELL_VOLUME + 2.0 * VISCOSITY
    known = [inertia * gas[c] + dep[2 + c] / CELL_VOLUME for c in range(3)]
    for s in range(CHUNKS):
        one = slice(s, s + 1)
        known_ref[s] = jnp.concatenate(
            [g[one] for g in gas] + [k[one] for k in known] + [diag[one], diag[one]], axis=0
        )
    low_ref[...] = known_ref[0]
    high_ref[...] = known_ref[CHUNKS - 1]


def sweeps_kernel(par_ref, near_ref, far_ref, known_ref, gas_out, table_ref):
    odd = par_ref[0] == 1
    below = jnp.where(odd, near_ref[...], far_ref[...])
    above = jnp.where(odd, far_ref[...], near_ref[...])
    full = jnp.concatenate([below] + [known_ref[s] for s in range(CHUNKS)] + [above], axis=1)
    width = full.shape[1]
    inverse = 1.0 / full[6:7]
    pad = jnp.zeros((5, width), F32)
    gas = jnp.concatenate([full[0:3], pad], axis=0)
    known = jnp.concatenate([full[3:6], pad], axis=0)
    for sweep in range(SWEEPS):
        sides = pltpu.roll(gas, 1, 1) + pltpu.roll(gas, width - 1, 1)
        gas = (known + VISCOSITY * sides) * inverse
    gas_out[...] = gas[0:3, BP : BP + CHUNKS * BP]
    for c in range(3):
        for s in range(CHUNKS):
            table_ref[c, s : s + 1, :] = gas[c : c + 1, (s + 1) * BP : (s + 2) * BP]


def pick_kernel(par_ref, owner_ref, cell_ref, mine_ref, other_ref, out_ref):
    par = par_ref[0]
    place_of = lax.broadcasted_iota(jnp.int32, (BP, BP), 0)
    quarter = lax.broadcasted_iota(jnp.int32, (CHUNKS, BP), 0)
    pad = jnp.zeros((4, BP), F32)
    for b in range(NB):
        cell = cell_ref[b : b + 1, :]
        chunk = cell // BP
        hot = jnp.where(place_of == cell % BP, 1.0, 0.0).astype(BF16)
        owner = owner_ref[b]
        chip = owner // 2
        mine = owner % 2 == par
        rows = [jnp.where(mine, mine_ref[chip, c], other_ref[chip, c]) for c in range(3)]
        rows = jnp.concatenate(rows + [pad], axis=0)
        stacked = jnp.concatenate(parts3(rows), axis=0).astype(BF16)
        found = jnp.dot(stacked, hot, preferred_element_type=F32)
        found = found[0:16] + found[16:32] + found[32:48]
        here = quarter == chunk
        out_ref[:, b * BP : (b + 1) * BP] = jnp.concatenate(
            [
                jnp.sum(jnp.where(here, found[4 * c : 4 * c + 4], 0.0), axis=0, keepdims=True)
                for c in range(3)
            ],
            axis=0,
        )


def swap_pairs(count):
    near = [(d, d ^ 1) for d in range(count)]
    far = [(d, (d + 1) % count if d % 2 else (d - 1) % count) for d in range(count)]
    return near, far


def body(
    positions,
    velocities,
    particle_volume,
    drag_coef,
    gas_at_particle,
    pair_first,
    pair_second,
    ghost_list,
    block_owner,
    cell_map,
    gas_velocity,
):
    axes = ("grp", "dom")
    ndom = lax.axis_size("dom")
    near_pairs, far_pairs = swap_pairs(lax.axis_size("grp") * ndom)

    def exchange(near, far):
        far = lax.ppermute(far, axes, far_pairs)
        near = lax.ppermute(near, axes, near_pairs)
        return near, far

    par = (lax.axis_index("dom") & 1).astype(jnp.int32).reshape(1)
    chips = ndom // 2
    same_core = [list(range(core, ndom, 2)) for core in range(2)]
    mass = particle_volume.reshape(NB, BP)
    beta = drag_coef.reshape(NB, BP)
    cells = cell_map.reshape(NB, BP)
    owner = block_owner.reshape(NB)

    state, aux, near, far, lists = prepare(
        par, ghost_list, positions, velocities, gas_at_particle, mass, beta, pair_first, pair_second
    )
    scalars = (par, ghost_list, lists, owner)
    rb = None
    for step in range(SUBSTEPS):
        near, far = exchange(near, far)
        part, g, rb = local_pairs(lists, state, rb)
        last = step == SUBSTEPS - 1
        outs = ghost_pairs(last, chips, scalars, cells, state, near, far, aux, part, g)
        if not last:
            state, near, far = outs
    pos_out, vel_out, keep, give = outs

    dep = keep + lax.ppermute(give, axes, near_pairs)
    dep = lax.all_to_all(dep, "dom", 0, 0, axis_index_groups=same_core, tiled=True)

    tile = jax.ShapeDtypeStruct((8, BP), F32)
    void, known, low, high = pl.pallas_call(
        known_kernel,
        in_specs=[VMEM] * 2,
        out_shape=(
            jax.ShapeDtypeStruct((CHUNKS, BP), F32),
            jax.ShapeDtypeStruct((CHUNKS, 8, BP), F32),
            tile,
            tile,
        ),
        out_specs=(VMEM,) * 4,
        compiler_params=PARAMS,
        cost_estimate=cost(400000, 700000),
        name="known",
    )(dep, gas_velocity)
    odd = par[0] == 1
    near, far = exchange(jnp.where(odd, low, high), jnp.where(odd, high, low))
    gas, table = pl.pallas_call(
        sweeps_kernel,
        in_specs=[SMEM] + [VMEM] * 3,
        out_shape=(
            jax.ShapeDtypeStruct((3, CHUNKS * BP), F32),
            jax.ShapeDtypeStruct((3, CHUNKS, BP), F32),
        ),
        out_specs=(VMEM,) * 2,
        compiler_params=PARAMS,
        cost_estimate=cost(40000, 50000),
        name="sweeps",
    )(par, near, far, known)

    table = jnp.broadcast_to(table[None], (chips, 3, CHUNKS, BP))
    table = lax.all_to_all(table, "dom", 0, 0, axis_index_groups=same_core, tiled=True)
    other = lax.ppermute(table, axes, near_pairs)
    particle_gas = pl.pallas_call(
        pick_kernel,
        in_specs=[SMEM] * 2 + [VMEM] * 3,
        out_shape=jax.ShapeDtypeStruct((3, NB * BP), F32),
        out_specs=VMEM,
        compiler_params=PARAMS,
        cost_estimate=cost(60000000, 900000),
        name="pick",
    )(par, owner, cells, table, other)
    return (pos_out, vel_out, gas, void.reshape(-1), particle_gas)


def solution(mesh):
    both = ("grp", "dom")
    return jax.shard_map(
        body,
        mesh=mesh,
        in_specs=(
            P(None, both),
            P(None, both),
            P(both),
            P(both),
            P(None, both),
            P(both),
            P(both),
            P(None, both),
            P(both, None),
            P(both),
            P(None, both),
        ),
        out_specs=(
            P(None, both),
            P(None, both),
            P(None, both),
            P(both),
            P(None, both),
        ),
        check_vma=False,
    )
```

```python
import functools

import jax
import jax.numpy as jnp
from jax import lax
from jax.experimental import pallas as pl
from jax.experimental.pallas import tpu as pltpu
from jax.sharding import PartitionSpec as P

NB = 32
BP = 128
NG = 2
NEXT = NB + 2 * NG
NPAIR = 128
GROUP = 8
SUBSTEPS = 4
SWEEPS = 4
K = 5
CHUNKS = 4
DEPROWS = 24
ROOM = NPAIR + 2 * GROUP
LISTS = 4 * ROOM + 8
PARITY, GHOST, OWNER, FIRST, SECOND = 0, 4, 8, 128, 256

SLAB = 4.0
SOFT = 0.01
STIFF = 20.0
STEP = 0.01
GRAVITY_Z = -1.0
RADIUS_FACTOR = 0.62
CELL_VOLUME = 16.0
RHO_STEP = 2.0
VISCOSITY = 1.0
TINY = 1e-36

F32 = jnp.float32
BF16 = jnp.bfloat16
VMEM = pl.BlockSpec(memory_space=pltpu.VMEM)
SMEM = pl.BlockSpec(memory_space=pltpu.SMEM)
PARAMS = pltpu.CompilerParams(vmem_limit_bytes=24 * 1024 * 1024)


def cost(flops, nbytes, transcendentals=0):
    return pl.CostEstimate(flops=flops, bytes_accessed=nbytes, transcendentals=transcendentals)


def parts3(value):
    high = value.astype(BF16).astype(F32)
    rest = value - high
    mid = rest.astype(BF16).astype(F32)
    low = (rest - mid).astype(BF16).astype(F32)
    return high, mid, low


def swap3(tile):
    return jnp.concatenate([tile[:, 3:6], tile[:, 0:3], tile[:, 6:8]], axis=1)


def fill_sends(int_ref, state_ref, near_ref, far_ref):
    par = int_ref[PARITY]
    for s in range(NG):
        near_ref[s] = state_ref[int_ref[GHOST + NG * par + s]]
        far_ref[s] = state_ref[int_ref[GHOST + NG * (1 - par) + s]]


def prepare_kernel(int_ref, in_ref, state_ref, aux_ref, near_ref, far_ref, list_ref):
    mass = jnp.concatenate([in_ref[9:10, b * BP : (b + 1) * BP] for b in range(NB)], axis=0)
    radius = RADIUS_FACTOR * jnp.exp(jnp.log(mass) * (1.0 / 3.0))
    zero3 = jnp.zeros((3, BP), F32)
    for b in range(NB):
        lanes = slice(b * BP, (b + 1) * BP)
        rows = slice(b, b + 1)
        state_ref[b] = jnp.concatenate(
            [in_ref[0:6, lanes], radius[rows], jnp.zeros((1, BP), F32)], axis=0
        )
        aux_ref[b] = jnp.concatenate([zero3, in_ref[6:9, lanes], in_ref[10:11, lanes], mass[rows]], axis=0)
    fill_sends(int_ref, state_ref, near_ref, far_ref)

    def sort_pair(p, counts):
        local, ghost = counts
        first = int_ref[FIRST + p]
        second = int_ref[SECOND + p]
        is_ghost = (second >= NB).astype(jnp.int32)
        slot = jnp.where(is_ghost == 1, 2 * ROOM + ghost, GROUP + local)
        list_ref[slot] = first
        list_ref[ROOM + slot] = second
        return local + 1 - is_ghost, ghost + is_ghost

    local, ghost = lax.fori_loop(0, NPAIR, sort_pair, (jnp.int32(0), jnp.int32(0)))
    for s in range(GROUP):
        list_ref[s] = NB
        list_ref[ROOM + s] = 0
        list_ref[GROUP + local + s] = NB
        list_ref[ROOM + GROUP + local + s] = 0
        list_ref[2 * ROOM + ghost + s] = NB
        list_ref[3 * ROOM + ghost + s] = NB
    list_ref[4 * ROOM] = (local + GROUP - 1) // GROUP
    list_ref[4 * ROOM + 1] = (ghost + GROUP - 1) // GROUP


def prepare(ints, floats):
    tile = jax.ShapeDtypeStruct((NB, 8, BP), F32)
    send = jax.ShapeDtypeStruct((NG, 8, BP), F32)
    lists = jax.ShapeDtypeStruct((LISTS,), jnp.int32)
    return pl.pallas_call(
        prepare_kernel,
        in_specs=[SMEM, VMEM],
        out_shape=(tile, tile, send, send, lists),
        out_specs=(VMEM,) * 4 + (SMEM,),
        compiler_params=PARAMS,
        cost_estimate=cost(100000, 600000),
        name="prepare",
    )(ints, floats)


def row_index():
    return lax.broadcasted_iota(jnp.int32, (8, BP), 0)[None]


def features(tile):
    row = row_index()
    swapped = swap3(tile)
    norm = jnp.sum(jnp.where(row < 3, tile * tile, 0.0), axis=1, keepdims=True)
    cross = jnp.sum(jnp.where(row < 3, tile * swapped, 0.0), axis=1, keepdims=True) * (1.0 / STIFF)
    return swapped, norm, cross


def partner_side(tile, base, jt_ref, a_ref):
    row = row_index()
    r = row[0]
    ones = jnp.ones((8, BP), F32)
    zeros = jnp.zeros((8, BP), F32)
    swapped, norm, cross = features(tile)
    full = jnp.where(row < 6, tile, jnp.where(row == 6, norm, cross))
    high, mid, low = parts3(full)
    is_v = (r >= 3) & (r < 6)
    for s in range(4):
        h, m, l = high[s], mid[s], low[s]
        stack = jnp.concatenate([h, h, h, m, m, l, ones, zeros], axis=0)
        jt_ref[base + s] = jnp.transpose(stack).astype(BF16)
        by_x = jnp.concatenate(
            [
                jnp.where(r < 3, h, jnp.where(r == 6, 1.0, 0.0)),
                jnp.where(r < 3, m, 0.0),
                jnp.where(r < 3, l, 0.0),
                zeros,
            ],
            axis=0,
        )
        by_v = jnp.concatenate(
            [
                jnp.where(is_v, h, jnp.where(r == 7, 1.0, 0.0)),
                jnp.where(is_v, m, 0.0),
                jnp.where(is_v, l, 0.0),
                zeros,
            ],
            axis=0,
        )
        a_ref[base + s] = jnp.concatenate([by_x, by_v], axis=1).astype(BF16)


def own_side(tile, base, g_ref):
    row = row_index()
    zeros = jnp.zeros((8, BP), F32)
    swapped, norm, cross = features(tile)
    xh, xm, xl = parts3(jnp.where(row < 3, -2.0 * tile, 0.0))
    xh = jnp.where(row == 6, 1.0, xh)
    vh, vm, vl = parts3(jnp.where(row < 6, swapped * (-1.0 / STIFF), 0.0))
    vh = jnp.where(row == 7, 1.0, vh)
    nh, nm, nl = parts3(norm + SOFT)
    ch, cm, cl = parts3(cross)
    own_n = jnp.where(row == 0, nh, jnp.where(row == 1, nm, jnp.where(row == 2, nl, 0.0)))
    own_c = jnp.where(row == 0, ch, jnp.where(row == 1, cm, jnp.where(row == 2, cl, 0.0)))
    for s in range(4):
        left = jnp.concatenate([xh[s], xm[s], xl[s], xh[s], xm[s], xh[s], own_n[s], zeros], axis=0)
        right = jnp.concatenate([vh[s], vm[s], vl[s], vh[s], vm[s], vh[s], own_c[s], zeros], axis=0)
        g_ref[base + s] = jnp.concatenate([left, right], axis=1).astype(BF16)


def pair_product(a, b, jt_ref, g_ref):
    return jnp.dot(jt_ref[b], g_ref[a], preferred_element_type=F32)


def pair_weights(both, a, b, state_ref, rb_ref):
    dist2 = both[:, :BP]
    slide = both[:, BP:]
    inv = lax.rsqrt(dist2)
    overlap = (rb_ref[b] + state_ref[a, 6:7, :]) - dist2 * inv
    delta = jnp.maximum(overlap, 0.0)
    root = delta * lax.rsqrt(jnp.maximum(overlap, TINY))
    push = (root * inv) * (delta - slide * inv)
    push_high = push.astype(BF16)
    push_low = (push - push_high.astype(F32)).astype(BF16)
    root_high = root.astype(BF16)
    root_low = (root - root_high.astype(F32)).astype(BF16)
    return jnp.concatenate([push_high, push_low, root_high, root_low], axis=0)


def partner_sums(partners, weights, a_ref):
    lefts = []
    for b in partners:
        left_x = a_ref[b, :, :BP]
        left_v = a_ref[b, :, BP:]
        lefts.append(jnp.concatenate([left_x, left_x, left_v, left_v], axis=1))
    sums = jnp.dot(jnp.concatenate(lefts, axis=0), jnp.concatenate(weights, axis=1), preferred_element_type=F32)
    one, two = sums[0:32, :BP], sums[32:64, BP:]
    return one[0:8] + one[8:16] + one[16:24], two[0:8] + two[8:16] + two[16:24]


def ghost_loop(groups, list_ref, acc_ref, state_ref, jt_ref, g_ref, a_ref, rb_ref):
    def group(k, carry):
        start = 2 * ROOM + k * GROUP
        firsts = [list_ref[start + s] for s in range(GROUP)]
        seconds = [list_ref[start + ROOM + s] - NB for s in range(GROUP)]
        weights = []
        for s in range(GROUP):
            a, b = jnp.minimum(firsts[s], NB - 1), seconds[s]
            weights.append(pair_weights(pair_product(a, b, jt_ref, g_ref), a, b, state_ref, rb_ref))
        sums = []
        for s in range(0, GROUP, 2):
            sums.extend(partner_sums(seconds[s : s + 2], weights[s : s + 2], a_ref))
        for a, value in zip(firsts, sums):
            acc_ref[a] += value
        return carry

    lax.fori_loop(0, groups, group, 0)


def local_loop(groups, list_ref, acc_ref, state_ref, jt_ref, g_ref, a_ref, rb_ref, held_ref):
    def finish(start, s):
        partners = [list_ref[ROOM + start + s + t] for t in range(2)]
        sums = partner_sums(partners, [held_ref[s], held_ref[s + 1]], a_ref)
        for t in range(2):
            acc_ref[list_ref[start + s + t]] += sums[t]

    def group(k, carry):
        start = k * GROUP
        for s in range(GROUP):
            a = jnp.minimum(list_ref[start + GROUP + s], NB - 1)
            b = list_ref[ROOM + start + GROUP + s]
            both = pair_product(a, b, jt_ref, g_ref)
            if s % 2 == 0:
                finish(start, s)
            held_ref[s] = pair_weights(both, a, b, state_ref, rb_ref)
        return carry

    held_ref[...] = jnp.zeros(held_ref.shape, BF16)
    lax.fori_loop(0, groups, group, 0)
    for s in range(0, GROUP, 2):
        finish(groups * GROUP, s)


def local_kernel(opening, *refs):
    if opening:
        list_ref, state_ref, acc_ref, g_ref, rb_ref, jt_ref, a_ref, held_ref = refs
        column = jnp.transpose(state_ref[:, 6, :])
        for b in range(NB):
            rb_ref[b] = jnp.broadcast_to(column[:, b : b + 1], (BP, BP))
    else:
        list_ref, state_ref, rb_ref, acc_ref, g_ref, jt_ref, a_ref, held_ref = refs

    def blocks(k, carry):
        tile = state_ref[pl.ds(k * 4, 4)]
        partner_side(tile, k * 4, jt_ref, a_ref)
        own_side(tile, k * 4, g_ref)
        return carry

    lax.fori_loop(0, NB // 4, blocks, 0)
    acc_ref[...] = jnp.zeros(acc_ref.shape, F32)
    local_loop(list_ref[4 * ROOM], list_ref, acc_ref, state_ref, jt_ref, g_ref, a_ref, rb_ref, held_ref)


def local_pairs(lists, state, rb=None):
    opening = rb is None
    outs = (
        jax.ShapeDtypeStruct((NB + 1, 8, BP), F32),
        jax.ShapeDtypeStruct((NB, 64, 2 * BP), BF16),
    )
    wide = (jax.ShapeDtypeStruct((NB, BP, BP), F32),)
    args = (lists, state) if opening else (lists, state, rb)
    outs = pl.pallas_call(
        functools.partial(local_kernel, opening),
        in_specs=[SMEM] + [VMEM] * (len(args) - 1),
        out_shape=outs + (wide if opening else ()),
        out_specs=(VMEM,) * (3 if opening else 2),
        scratch_shapes=[
            pltpu.VMEM((NB, BP, 64), BF16),
            pltpu.VMEM((NB, 32, 2 * BP), BF16),
            pltpu.VMEM((GROUP, 4 * BP, BP), BF16),
        ],
        compiler_params=PARAMS,
        cost_estimate=cost(10000000000, 3500000, 4000000),
        name="local_pairs",
    )(*args)
    return outs if opening else (*outs, rb)


def ghost_kernel(last, *refs):
    (int_ref, list_ref), refs = refs[:2], refs[2:]
    (cell_ref, state_ref, near_in, far_in, aux_ref, part_ref, g_ref), refs = refs[:7], refs[7:]
    if last:
        (pos_out, vel_out, keep_ref, give_ref), (*scratch, spread_ref) = refs[:4], refs[4:]
    else:
        (new_ref, near_out, far_out), scratch = refs[:3], refs[3:]
    ext_ref, jt_ref, a_ref, rb_ref, acc_ref = scratch
    par = int_ref[PARITY]
    row = row_index()

    sign = 1.0 - 2.0 * par.astype(F32)
    shift = jnp.where(row[0] == 0, SLAB * sign, 0.0)
    for s in range(NG):
        ext_ref[NG * (1 - par) + s] = near_in[s] + shift
        ext_ref[NG * par + s] = far_in[s] - shift
    for s in range(2 * NG, 8):
        ext_ref[s] = jnp.zeros((8, BP), F32)
    column = jnp.transpose(ext_ref[:, 6, :])
    for b in range(2 * NG):
        rb_ref[b] = jnp.broadcast_to(column[:, b : b + 1], (BP, BP))
    partner_side(ext_ref[0:4], 0, jt_ref, a_ref)
    acc_ref[...] = part_ref[...]
    ghost_loop(list_ref[4 * ROOM + 1], list_ref, acc_ref, state_ref, jt_ref, g_ref, a_ref, rb_ref)

    tile = state_ref[...]
    acc = acc_ref[0:NB]
    aux = aux_ref[...]
    by_x = STIFF * (tile * acc[:, 6:7] - acc)
    by_v = acc - tile * acc[:, 7:8]
    force = swap3(by_x) + by_v
    beta = aux[:, 6:7]
    mass = aux[:, 7:8]
    gravity = jnp.where(row == 5, GRAVITY_Z, 0.0)
    velocity = tile + STEP * ((force + beta * (aux - tile)) / mass + gravity)
    place = tile + STEP * swap3(velocity)
    moved = jnp.where(row < 3, place, jnp.where(row < 6, velocity, tile))

    if not last:
        new_ref[...] = moved
        fill_sends(int_ref, new_ref, near_out, far_out)
        return

    for b in range(NB):
        lanes = slice(b * BP, (b + 1) * BP)
        pos_out[:, lanes] = moved[b, 0:3]
        vel_out[:, lanes] = moved[b, 3:6]

    keep_ref[...] = jnp.zeros(keep_ref.shape, F32)
    give_ref[...] = jnp.zeros(give_ref.shape, F32)
    drag = beta * moved
    quarter = lax.broadcasted_iota(jnp.int32, (DEPROWS, BP), 0) % CHUNKS
    place_of = lax.broadcasted_iota(jnp.int32, (BP, BP), 0)
    zeros = jnp.zeros((8, BP), F32)
    tail = jnp.zeros((DEPROWS - CHUNKS * K, BP), F32)
    for b in range(NB):
        cell = cell_ref[b : b + 1, :]
        chunk = cell // BP
        hot = jnp.where(place_of == cell % BP, 1.0, 0.0).astype(BF16)
        values = [mass[b], beta[b], drag[b, 3:4], drag[b, 4:5], drag[b, 5:6]]
        amounts = jnp.concatenate([jnp.broadcast_to(v, (CHUNKS, BP)) for v in values] + [tail], axis=0)
        amounts = jnp.where(quarter == chunk, amounts, 0.0)
        stacked = jnp.concatenate(list(parts3(amounts)) + [zeros], axis=0).astype(BF16)
        spread = lax.dot_general(stacked, hot, (((1,), (1,)), ((), ())), preferred_element_type=F32)
        spread_ref[b] = spread[0:DEPROWS] + spread[DEPROWS : 2 * DEPROWS] + spread[2 * DEPROWS : 3 * DEPROWS]

    for b in range(NB):
        owner = int_ref[OWNER + b]

        def put(target, b=b, chip=owner // 2):
            for q in range(K):
                target[chip, q] += spread_ref[b, CHUNKS * q : CHUNKS * (q + 1)]

        mine = owner % 2 == par
        pl.when(mine)(functools.partial(put, keep_ref))
        pl.when(jnp.logical_not(mine))(functools.partial(put, give_ref))


def ghost_pairs(last, chips, scalars, cells, state, near, far, aux, part, g):
    tile = jax.ShapeDtypeStruct((NB, 8, BP), F32)
    send = jax.ShapeDtypeStruct((NG, 8, BP), F32)
    if last:
        flat = jax.ShapeDtypeStruct((3, NB * BP), F32)
        dep = jax.ShapeDtypeStruct((chips, K, CHUNKS, BP), F32)
        outs = (flat, flat, dep, dep)
    else:
        outs = (tile, send, send)
    return pl.pallas_call(
        functools.partial(ghost_kernel, last),
        in_specs=[SMEM] * 2 + [VMEM] * 7,
        out_shape=outs,
        out_specs=(VMEM,) * len(outs),
        scratch_shapes=[
            pltpu.VMEM((8, 8, BP), F32),
            pltpu.VMEM((2 * NG, BP, 64), BF16),
            pltpu.VMEM((2 * NG, 32, 2 * BP), BF16),
            pltpu.VMEM((2 * NG, BP, BP), F32),
            pltpu.VMEM((NB + 1, 8, BP), F32),
        ]
        + ([pltpu.VMEM((NB, DEPROWS, BP), F32)] if last else []),
        compiler_params=PARAMS,
        cost_estimate=cost(2000000000, 2000000, 500000),
        name="ghost_pairs_last" if last else "ghost_pairs",
    )(*scalars, cells, state, near, far, aux, part, g)


def known_kernel(dep_ref, gas_ref, void_ref, known_ref, low_ref, high_ref):
    dep = jnp.sum(dep_ref[...], axis=0)
    void = CELL_VOLUME / (CELL_VOLUME + dep[0])
    inertia = RHO_STEP * void
    void_ref[...] = void
    gas = [
        jnp.concatenate([gas_ref[c : c + 1, s * BP : (s + 1) * BP] for s in range(CHUNKS)], axis=0)
        for c in range(3)
    ]
    diag = inertia + dep[1] / CELL_VOLUME + 2.0 * VISCOSITY
    known = [inertia * gas[c] + dep[2 + c] / CELL_VOLUME for c in range(3)]
    for s in range(CHUNKS):
        one = slice(s, s + 1)
        known_ref[s] = jnp.concatenate(
            [g[one] for g in gas] + [k[one] for k in known] + [diag[one], diag[one]], axis=0
        )
    low_ref[...] = known_ref[0]
    high_ref[...] = known_ref[CHUNKS - 1]


def sweeps_kernel(int_ref, near_ref, far_ref, known_ref, gas_out, table_ref):
    odd = int_ref[PARITY] == 1
    below = jnp.where(odd, near_ref[...], far_ref[...])
    above = jnp.where(odd, far_ref[...], near_ref[...])
    full = jnp.concatenate([below] + [known_ref[s] for s in range(CHUNKS)] + [above], axis=1)
    width = full.shape[1]
    inverse = 1.0 / full[6:7]
    pad = jnp.zeros((5, width), F32)
    gas = jnp.concatenate([full[0:3], pad], axis=0)
    known = jnp.concatenate([full[3:6], pad], axis=0)
    for sweep in range(SWEEPS):
        sides = pltpu.roll(gas, 1, 1) + pltpu.roll(gas, width - 1, 1)
        gas = (known + VISCOSITY * sides) * inverse
    gas_out[...] = gas[0:3, BP : BP + CHUNKS * BP]
    for c in range(3):
        for s in range(CHUNKS):
            table_ref[c, s : s + 1, :] = gas[c : c + 1, (s + 1) * BP : (s + 2) * BP]


def pick_kernel(int_ref, cell_ref, mine_ref, other_ref, out_ref):
    par = int_ref[PARITY]
    place_of = lax.broadcasted_iota(jnp.int32, (BP, BP), 0)
    quarter = lax.broadcasted_iota(jnp.int32, (CHUNKS, BP), 0)
    pad = jnp.zeros((4, BP), F32)
    for b in range(NB):
        cell = cell_ref[b : b + 1, :]
        chunk = cell // BP
        hot = jnp.where(place_of == cell % BP, 1.0, 0.0).astype(BF16)
        owner = int_ref[OWNER + b]
        chip = owner // 2
        mine = owner % 2 == par
        rows = [jnp.where(mine, mine_ref[chip, c], other_ref[chip, c]) for c in range(3)]
        rows = jnp.concatenate(rows + [pad], axis=0)
        stacked = jnp.concatenate(parts3(rows), axis=0).astype(BF16)
        found = jnp.dot(stacked, hot, preferred_element_type=F32)
        found = found[0:16] + found[16:32] + found[32:48]
        here = quarter == chunk
        out_ref[:, b * BP : (b + 1) * BP] = jnp.concatenate(
            [
                jnp.sum(jnp.where(here, found[4 * c : 4 * c + 4], 0.0), axis=0, keepdims=True)
                for c in range(3)
            ],
            axis=0,
        )


def swap_pairs(count):
    near = [(d, d ^ 1) for d in range(count)]
    far = [(d, (d + 1) % count if d % 2 else (d - 1) % count) for d in range(count)]
    return near, far


def body(
    positions,
    velocities,
    particle_volume,
    drag_coef,
    gas_at_particle,
    pair_first,
    pair_second,
    ghost_list,
    block_owner,
    cell_map,
    gas_velocity,
):
    axes = ("grp", "dom")
    ndom = lax.axis_size("dom")
    near_pairs, far_pairs = swap_pairs(lax.axis_size("grp") * ndom)

    def exchange(near, far):
        far = lax.ppermute(far, axes, far_pairs)
        near = lax.ppermute(near, axes, near_pairs)
        return near, far

    par = (lax.axis_index("dom") & 1).astype(jnp.int32).reshape(1)
    chips = ndom // 2
    same_core = [list(range(core, ndom, 2)) for core in range(2)]
    cells = cell_map.reshape(NB, BP)
    pad = jnp.zeros((3,), jnp.int32)
    ints = [par, pad, ghost_list.reshape(-1), block_owner.reshape(-1), jnp.zeros((FIRST - OWNER - NB,), jnp.int32)]
    ints = jnp.concatenate(ints + [pair_first, pair_second])
    floats = jnp.concatenate(
        [positions, velocities, gas_at_particle, particle_volume[None], drag_coef[None]], axis=0
    )

    state, aux, near, far, lists = prepare(ints, floats)
    scalars = (ints, lists)
    rb = None
    for step in range(SUBSTEPS):
        near, far = exchange(near, far)
        part, g, rb = local_pairs(lists, state, rb)
        last = step == SUBSTEPS - 1
        outs = ghost_pairs(last, chips, scalars, cells, state, near, far, aux, part, g)
        if not last:
            state, near, far = outs
    pos_out, vel_out, keep, give = outs

    dep = keep + lax.ppermute(give, axes, near_pairs)
    dep = lax.all_to_all(dep, "dom", 0, 0, axis_index_groups=same_core, tiled=True)

    tile = jax.ShapeDtypeStruct((8, BP), F32)
    void, known, low, high = pl.pallas_call(
        known_kernel,
        in_specs=[VMEM] * 2,
        out_shape=(
            jax.ShapeDtypeStruct((CHUNKS, BP), F32),
            jax.ShapeDtypeStruct((CHUNKS, 8, BP), F32),
            tile,
            tile,
        ),
        out_specs=(VMEM,) * 4,
        compiler_params=PARAMS,
        cost_estimate=cost(400000, 700000),
        name="known",
    )(dep, gas_velocity)
    odd = par[0] == 1
    near, far = exchange(jnp.where(odd, low, high), jnp.where(odd, high, low))
    gas, table = pl.pallas_call(
        sweeps_kernel,
        in_specs=[SMEM] + [VMEM] * 3,
        out_shape=(
            jax.ShapeDtypeStruct((3, CHUNKS * BP), F32),
            jax.ShapeDtypeStruct((3, CHUNKS, BP), F32),
        ),
        out_specs=(VMEM,) * 2,
        compiler_params=PARAMS,
        cost_estimate=cost(40000, 50000),
        name="sweeps",
    )(ints, near, far, known)

    table = jnp.broadcast_to(table[None], (chips, 3, CHUNKS, BP))
    table = lax.all_to_all(table, "dom", 0, 0, axis_index_groups=same_core, tiled=True)
    other = lax.ppermute(table, axes, near_pairs)
    particle_gas = pl.pallas_call(
        pick_kernel,
        in_specs=[SMEM] + [VMEM] * 3,
        out_shape=jax.ShapeDtypeStruct((3, NB * BP), F32),
        out_specs=VMEM,
        compiler_params=PARAMS,
        cost_estimate=cost(60000000, 900000),
        name="pick",
    )(ints, cells, table, other)
    return (pos_out, vel_out, gas, void.reshape(-1), particle_gas)


def solution(mesh):
    both = ("grp", "dom")
    return jax.shard_map(
        body,
        mesh=mesh,
        in_specs=(
            P(None, both),
            P(None, both),
            P(both),
            P(both),
            P(None, both),
            P(both),
            P(both),
            P(None, both),
            P(both, None),
            P(both),
            P(None, both),
        ),
        out_specs=(
            P(None, both),
            P(None, both),
            P(None, both),
            P(both),
            P(None, both),
        ),
        check_vma=False,
    )
```

```python
import functools

import jax
import jax.numpy as jnp
from jax import lax
from jax.experimental import pallas as pl
from jax.experimental.pallas import tpu as pltpu
from jax.sharding import PartitionSpec as P

NB = 32
BP = 128
NG = 2
NEXT = NB + 2 * NG
NPAIR = 128
GROUP = 8
SUBSTEPS = 4
SWEEPS = 4
K = 5
CHUNKS = 4
DEPROWS = 24
ROOM = NPAIR + 3 * GROUP
STRIP = 32
LISTS = 4 * ROOM + 8

SLAB = 4.0
SOFT = 0.01
STIFF = 20.0
STEP = 0.01
GRAVITY_Z = -1.0
RADIUS_FACTOR = 0.62
CELL_VOLUME = 16.0
RHO_STEP = 2.0
VISCOSITY = 1.0
TINY = 1e-36

F32 = jnp.float32
BF16 = jnp.bfloat16
VMEM = pl.BlockSpec(memory_space=pltpu.VMEM)
SMEM = pl.BlockSpec(memory_space=pltpu.SMEM)
PARAMS = pltpu.CompilerParams(vmem_limit_bytes=24 * 1024 * 1024)


def cost(flops, nbytes, transcendentals=0):
    return pl.CostEstimate(flops=flops, bytes_accessed=nbytes, transcendentals=transcendentals)


def parts3(value):
    high = value.astype(BF16).astype(F32)
    rest = value - high
    mid = rest.astype(BF16).astype(F32)
    low = (rest - mid).astype(BF16).astype(F32)
    return high, mid, low


def swap3(tile):
    return jnp.concatenate([tile[:, 3:6], tile[:, 0:3], tile[:, 6:8]], axis=1)


def fill_sends(par_ref, ghost_ref, state_ref, near_ref, far_ref):
    par = par_ref[0]
    for s in range(NG):
        near_ref[s] = state_ref[ghost_ref[par, s]]
        far_ref[s] = state_ref[ghost_ref[1 - par, s]]


def prepare_kernel(
    par_ref, ghost_hbm, pos_hbm, vel_hbm, gas_hbm, mass_hbm, beta_hbm, first_hbm, second_hbm,
    state_ref, aux_ref, near_ref, far_ref, list_ref,
    ghost_ref, pos_ref, vel_ref, gas_ref, mass_ref, beta_ref, first_ref, second_ref, sems,
):
    sources = (ghost_hbm, pos_hbm, vel_hbm, gas_hbm, mass_hbm, beta_hbm, first_hbm, second_hbm)
    targets = (ghost_ref, pos_ref, vel_ref, gas_ref, mass_ref, beta_ref, first_ref, second_ref)
    copies = [pltpu.make_async_copy(s, t, sems.at[i]) for i, (s, t) in enumerate(zip(sources, targets))]
    for copy in copies:
        copy.start()
    for copy in copies:
        copy.wait()
    radius = RADIUS_FACTOR * jnp.exp(jnp.log(mass_ref[...]) * (1.0 / 3.0))
    zero3 = jnp.zeros((3, BP), F32)
    for b in range(NB):
        lanes = slice(b * BP, (b + 1) * BP)
        rows = slice(b, b + 1)
        state_ref[b] = jnp.concatenate(
            [pos_ref[:, lanes], vel_ref[:, lanes], radius[rows], jnp.zeros((1, BP), F32)], axis=0
        )
        aux_ref[b] = jnp.concatenate([zero3, gas_ref[:, lanes], beta_ref[rows], mass_ref[rows]], axis=0)
    fill_sends(par_ref, ghost_ref, state_ref, near_ref, far_ref)

    def sort_pair(p, counts):
        local, ghost = counts
        first = first_ref[p]
        second = second_ref[p]
        is_ghost = (second >= NB).astype(jnp.int32)
        slot = jnp.where(is_ghost == 1, 2 * ROOM + ghost, GROUP + local)
        list_ref[slot] = first
        list_ref[ROOM + slot] = second
        return local + 1 - is_ghost, ghost + is_ghost

    local, ghost = lax.fori_loop(0, NPAIR, sort_pair, (jnp.int32(0), jnp.int32(0)))
    for s in range(GROUP):
        list_ref[s] = NB
        list_ref[ROOM + s] = 0
        list_ref[GROUP + local + s] = NB
        list_ref[ROOM + GROUP + local + s] = 0
        list_ref[2 * GROUP + local + s] = NB
        list_ref[ROOM + 2 * GROUP + local + s] = 0
        list_ref[2 * ROOM + ghost + s] = NB
        list_ref[3 * ROOM + ghost + s] = NB
    list_ref[4 * ROOM] = (local + GROUP - 1) // GROUP
    list_ref[4 * ROOM + 1] = (ghost + GROUP - 1) // GROUP


def prepare(par, ghost_list, pos, vel, gas_seen, mass, beta, first, second):
    tile = jax.ShapeDtypeStruct((NB, 8, BP), F32)
    send = jax.ShapeDtypeStruct((NG, 8, BP), F32)
    lists = jax.ShapeDtypeStruct((LISTS,), jnp.int32)
    return pl.pallas_call(
        prepare_kernel,
        in_specs=[SMEM] + [pl.BlockSpec(memory_space=pl.ANY)] * 8,
        out_shape=(tile, tile, send, send, lists),
        out_specs=(VMEM,) * 4 + (SMEM,),
        scratch_shapes=[
            pltpu.SMEM((2, NG), jnp.int32),
            pltpu.VMEM((3, NB * BP), F32),
            pltpu.VMEM((3, NB * BP), F32),
            pltpu.VMEM((3, NB * BP), F32),
            pltpu.VMEM((NB, BP), F32),
            pltpu.VMEM((NB, BP), F32),
            pltpu.SMEM((NPAIR,), jnp.int32),
            pltpu.SMEM((NPAIR,), jnp.int32),
            pltpu.SemaphoreType.DMA((8,)),
        ],
        compiler_params=pltpu.CompilerParams(vmem_limit_bytes=58 * 1024 * 1024),
        cost_estimate=cost(100000, 600000),
        name="prepare",
    )(par, ghost_list, pos, vel, gas_seen, mass, beta, first, second)


def row_index():
    return lax.broadcasted_iota(jnp.int32, (8, BP), 0)[None]


def features(tile):
    row = row_index()
    swapped = swap3(tile)
    norm = jnp.sum(jnp.where(row < 3, tile * tile, 0.0), axis=1, keepdims=True)
    cross = jnp.sum(jnp.where(row < 3, tile * swapped, 0.0), axis=1, keepdims=True) * (1.0 / STIFF)
    return swapped, norm, cross


def partner_side(tile, base, jt_ref, a_ref):
    row = row_index()
    r = row[0]
    ones = jnp.ones((8, BP), F32)
    zeros = jnp.zeros((8, BP), F32)
    swapped, norm, cross = features(tile)
    full = jnp.where(row < 6, tile, jnp.where(row == 6, norm, cross))
    high, mid, low = parts3(full)
    is_v = (r >= 3) & (r < 6)
    for s in range(4):
        h, m, l = high[s], mid[s], low[s]
        stack = jnp.concatenate([h, h, h, m, m, l, ones, zeros], axis=0)
        jt_ref[base + s] = jnp.transpose(stack).astype(BF16)
        by_x = jnp.concatenate(
            [
                jnp.where(r < 3, h, jnp.where(r == 6, 1.0, 0.0)),
                jnp.where(r < 3, m, 0.0),
                jnp.where(r < 3, l, 0.0),
                zeros,
            ],
            axis=0,
        )
        by_v = jnp.concatenate(
            [
                jnp.where(is_v, h, jnp.where(r == 7, 1.0, 0.0)),
                jnp.where(is_v, m, 0.0),
                jnp.where(is_v, l, 0.0),
                zeros,
            ],
            axis=0,
        )
        a_ref[base + s] = jnp.concatenate([by_x, by_v], axis=1).astype(BF16)


def own_side(tile, base, g_ref):
    row = row_index()
    zeros = jnp.zeros((8, BP), F32)
    swapped, norm, cross = features(tile)
    xh, xm, xl = parts3(jnp.where(row < 3, -2.0 * tile, 0.0))
    xh = jnp.where(row == 6, 1.0, xh)
    vh, vm, vl = parts3(jnp.where(row < 6, swapped * (-1.0 / STIFF), 0.0))
    vh = jnp.where(row == 7, 1.0, vh)
    nh, nm, nl = parts3(norm + SOFT)
    ch, cm, cl = parts3(cross)
    own_n = jnp.where(row == 0, nh, jnp.where(row == 1, nm, jnp.where(row == 2, nl, 0.0)))
    own_c = jnp.where(row == 0, ch, jnp.where(row == 1, cm, jnp.where(row == 2, cl, 0.0)))
    for s in range(4):
        left = jnp.concatenate([xh[s], xm[s], xl[s], xh[s], xm[s], xh[s], own_n[s], zeros], axis=0)
        right = jnp.concatenate([vh[s], vm[s], vl[s], vh[s], vm[s], vh[s], own_c[s], zeros], axis=0)
        g_ref[base + s] = jnp.concatenate([left, right], axis=1).astype(BF16)


def pair_product(a, b, jt_ref, g_ref):
    return jnp.dot(jt_ref[b], g_ref[a], preferred_element_type=F32)


def pair_weights(s, a, b, state_ref, rb_ref, product_ref, held_ref):
    radius = state_ref[a, 6:7, :]
    for c in range(0, BP, STRIP):
        rows = slice(c, c + STRIP)
        dist2 = product_ref[s, rows, :BP]
        slide = product_ref[s, rows, BP:]
        inv = lax.rsqrt(dist2)
        overlap = (rb_ref[b, rows, :] + radius) - dist2 * inv
        delta = jnp.maximum(overlap, 0.0)
        root = delta * lax.rsqrt(jnp.maximum(overlap, TINY))
        push = (root * inv) * (delta - slide * inv)
        push_high = push.astype(BF16)
        root_high = root.astype(BF16)
        held_ref[s, c : c + STRIP] = push_high
        held_ref[s, BP + c : BP + c + STRIP] = (push - push_high.astype(F32)).astype(BF16)
        held_ref[s, 2 * BP + c : 2 * BP + c + STRIP] = root_high
        held_ref[s, 3 * BP + c : 3 * BP + c + STRIP] = (root - root_high.astype(F32)).astype(BF16)


def partner_sums(s, a, b, a_ref, held_ref, acc_ref):
    left_x = a_ref[b, :, :BP]
    left_v = a_ref[b, :, BP:]
    left = jnp.concatenate([left_x, left_x, left_v, left_v], axis=1)
    sums = jnp.dot(left, held_ref[s], preferred_element_type=F32)
    acc_ref[a] += sums[0:8] + sums[8:16] + sums[16:24]


def ghost_loop(groups, list_ref, acc_ref, state_ref, jt_ref, g_ref, a_ref, rb_ref, product_ref, held_ref):
    def group(k, carry):
        start = 2 * ROOM + k * GROUP
        firsts = [list_ref[start + s] for s in range(GROUP)]
        owns = [jnp.minimum(a, NB - 1) for a in firsts]
        seconds = [list_ref[start + ROOM + s] - NB for s in range(GROUP)]
        for s in range(GROUP):
            product_ref[s] = pair_product(owns[s], seconds[s], jt_ref, g_ref)
        for s in range(GROUP):
            pair_weights(s, owns[s], seconds[s], state_ref, rb_ref, product_ref, held_ref)
        for s in range(GROUP):
            partner_sums(s, firsts[s], seconds[s], a_ref, held_ref, acc_ref)
        return carry

    lax.fori_loop(0, groups, group, 0)


def local_loop(groups, list_ref, acc_ref, state_ref, jt_ref, g_ref, a_ref, rb_ref, product_ref, held_ref):
    def pair(entry):
        return list_ref[entry], list_ref[ROOM + entry]

    def product(entry, s):
        a, b = pair(entry + s)
        product_ref[s] = pair_product(jnp.minimum(a, NB - 1), b, jt_ref, g_ref)

    def weights(entry, s):
        a, b = pair(entry + s)
        pair_weights(s, jnp.minimum(a, NB - 1), b, state_ref, rb_ref, product_ref, held_ref)

    def sums(entry, s):
        a, b = pair(entry + s)
        partner_sums(s, a, b, a_ref, held_ref, acc_ref)

    def group(k, carry):
        start = k * GROUP
        for s in range(GROUP):
            sums(start, s)
            weights(start + GROUP, s)
            product(start + 2 * GROUP, s)
        return carry

    held_ref[...] = jnp.zeros(held_ref.shape, BF16)
    for s in range(GROUP):
        product(GROUP, s)
    lax.fori_loop(0, groups, group, 0)
    for s in range(GROUP):
        sums(groups * GROUP, s)


def local_kernel(opening, *refs):
    if opening:
        list_ref, state_ref, acc_ref, g_ref, rb_ref, *scratch = refs
        column = jnp.transpose(state_ref[:, 6, :])
        for b in range(NB):
            rb_ref[b] = jnp.broadcast_to(column[:, b : b + 1], (BP, BP))
    else:
        list_ref, state_ref, rb_ref, acc_ref, g_ref, *scratch = refs

    jt_ref, a_ref, product_ref, held_ref = scratch

    def blocks(k, carry):
        tile = state_ref[pl.ds(k * 4, 4)]
        partner_side(tile, k * 4, jt_ref, a_ref)
        own_side(tile, k * 4, g_ref)
        return carry

    lax.fori_loop(0, NB // 4, blocks, 0)
    acc_ref[...] = jnp.zeros(acc_ref.shape, F32)
    local_loop(
        list_ref[4 * ROOM], list_ref, acc_ref, state_ref, jt_ref, g_ref, a_ref, rb_ref, product_ref, held_ref
    )


def local_pairs(lists, state, rb=None):
    opening = rb is None
    outs = (
        jax.ShapeDtypeStruct((NB + 1, 8, BP), F32),
        jax.ShapeDtypeStruct((NB, 64, 2 * BP), BF16),
    )
    wide = (jax.ShapeDtypeStruct((NB, BP, BP), F32),)
    args = (lists, state) if opening else (lists, state, rb)
    outs = pl.pallas_call(
        functools.partial(local_kernel, opening),
        in_specs=[SMEM] + [VMEM] * (len(args) - 1),
        out_shape=outs + (wide if opening else ()),
        out_specs=(VMEM,) * (3 if opening else 2),
        scratch_shapes=[
            pltpu.VMEM((NB, BP, 64), BF16),
            pltpu.VMEM((NB, 32, 2 * BP), BF16),
            pltpu.VMEM((GROUP, BP, 2 * BP), F32),
            pltpu.VMEM((GROUP, 4 * BP, BP), BF16),
        ],
        compiler_params=PARAMS,
        cost_estimate=cost(10000000000, 3500000, 4000000),
        name="local_pairs",
    )(*args)
    return outs if opening else (*outs, rb)


def ghost_kernel(last, *refs):
    (par_ref, ghost_ref, list_ref, owner_ref), refs = refs[:4], refs[4:]
    (cell_ref, state_ref, near_in, far_in, aux_ref, part_ref, g_ref), refs = refs[:7], refs[7:]
    if last:
        (pos_out, vel_out, keep_ref, give_ref), (*scratch, spread_ref) = refs[:4], refs[4:]
    else:
        (new_ref, near_out, far_out), scratch = refs[:3], refs[3:]
    ext_ref, jt_ref, a_ref, rb_ref, acc_ref, product_ref, held_ref = scratch
    par = par_ref[0]
    row = row_index()

    sign = 1.0 - 2.0 * par.astype(F32)
    shift = jnp.where(row[0] == 0, SLAB * sign, 0.0)
    for s in range(NG):
        ext_ref[NG * (1 - par) + s] = near_in[s] + shift
        ext_ref[NG * par + s] = far_in[s] - shift
    for s in range(2 * NG, 8):
        ext_ref[s] = jnp.zeros((8, BP), F32)
    column = jnp.transpose(ext_ref[:, 6, :])
    for b in range(2 * NG):
        rb_ref[b] = jnp.broadcast_to(column[:, b : b + 1], (BP, BP))
    partner_side(ext_ref[0:4], 0, jt_ref, a_ref)
    acc_ref[...] = part_ref[...]
    ghost_loop(
        list_ref[4 * ROOM + 1], list_ref, acc_ref, state_ref, jt_ref, g_ref, a_ref, rb_ref, product_ref, held_ref
    )

    tile = state_ref[...]
    acc = acc_ref[0:NB]
    aux = aux_ref[...]
    by_x = STIFF * (tile * acc[:, 6:7] - acc)
    by_v = acc - tile * acc[:, 7:8]
    force = swap3(by_x) + by_v
    beta = aux[:, 6:7]
    mass = aux[:, 7:8]
    gravity = jnp.where(row == 5, GRAVITY_Z, 0.0)
    velocity = tile + STEP * ((force + beta * (aux - tile)) / mass + gravity)
    place = tile + STEP * swap3(velocity)
    moved = jnp.where(row < 3, place, jnp.where(row < 6, velocity, tile))

    if not last:
        new_ref[...] = moved
        fill_sends(par_ref, ghost_ref, new_ref, near_out, far_out)
        return

    for b in range(NB):
        lanes = slice(b * BP, (b + 1) * BP)
        pos_out[:, lanes] = moved[b, 0:3]
        vel_out[:, lanes] = moved[b, 3:6]

    keep_ref[...] = jnp.zeros(keep_ref.shape, F32)
    give_ref[...] = jnp.zeros(give_ref.shape, F32)
    drag = beta * moved
    quarter = lax.broadcasted_iota(jnp.int32, (DEPROWS, BP), 0) % CHUNKS
    place_of = lax.broadcasted_iota(jnp.int32, (BP, BP), 0)
    zeros = jnp.zeros((8, BP), F32)
    tail = jnp.zeros((DEPROWS - CHUNKS * K, BP), F32)
    for b in range(NB):
        cell = cell_ref[b : b + 1, :]
        chunk = cell // BP
        hot = jnp.where(place_of == cell % BP, 1.0, 0.0).astype(BF16)
        values = [mass[b], beta[b], drag[b, 3:4], drag[b, 4:5], drag[b, 5:6]]
        amounts = jnp.concatenate([jnp.broadcast_to(v, (CHUNKS, BP)) for v in values] + [tail], axis=0)
        amounts = jnp.where(quarter == chunk, amounts, 0.0)
        stacked = jnp.concatenate(list(parts3(amounts)) + [zeros], axis=0).astype(BF16)
        spread = lax.dot_general(stacked, hot, (((1,), (1,)), ((), ())), preferred_element_type=F32)
        spread_ref[b] = spread[0:DEPROWS] + spread[DEPROWS : 2 * DEPROWS] + spread[2 * DEPROWS : 3 * DEPROWS]

    for b in range(NB):
        owner = owner_ref[b]

        def put(target, b=b, chip=owner // 2):
            for q in range(K):
                target[chip, q] += spread_ref[b, CHUNKS * q : CHUNKS * (q + 1)]

        mine = owner % 2 == par
        pl.when(mine)(functools.partial(put, keep_ref))
        pl.when(jnp.logical_not(mine))(functools.partial(put, give_ref))


def ghost_pairs(last, chips, scalars, cells, state, near, far, aux, part, g):
    tile = jax.ShapeDtypeStruct((NB, 8, BP), F32)
    send = jax.ShapeDtypeStruct((NG, 8, BP), F32)
    if last:
        flat = jax.ShapeDtypeStruct((3, NB * BP), F32)
        dep = jax.ShapeDtypeStruct((chips, K, CHUNKS, BP), F32)
        outs = (flat, flat, dep, dep)
    else:
        outs = (tile, send, send)
    return pl.pallas_call(
        functools.partial(ghost_kernel, last),
        in_specs=[SMEM] * 4 + [VMEM] * 7,
        out_shape=outs,
        out_specs=(VMEM,) * len(outs),
        scratch_shapes=[
            pltpu.VMEM((8, 8, BP), F32),
            pltpu.VMEM((2 * NG, BP, 64), BF16),
            pltpu.VMEM((2 * NG, 32, 2 * BP), BF16),
            pltpu.VMEM((2 * NG, BP, BP), F32),
            pltpu.VMEM((NB + 1, 8, BP), F32),
            pltpu.VMEM((GROUP, BP, 2 * BP), F32),
            pltpu.VMEM((GROUP, 4 * BP, BP), BF16),
        ]
        + ([pltpu.VMEM((NB, DEPROWS, BP), F32)] if last else []),
        compiler_params=PARAMS,
        cost_estimate=cost(2000000000, 2000000, 500000),
        name="ghost_pairs_last" if last else "ghost_pairs",
    )(*scalars, cells, state, near, far, aux, part, g)


def known_kernel(dep_ref, gas_ref, void_ref, known_ref, low_ref, high_ref):
    dep = jnp.sum(dep_ref[...], axis=0)
    void = CELL_VOLUME / (CELL_VOLUME + dep[0])
    inertia = RHO_STEP * void
    void_ref[...] = void
    gas = [
        jnp.concatenate([gas_ref[c : c + 1, s * BP : (s + 1) * BP] for s in range(CHUNKS)], axis=0)
        for c in range(3)
    ]
    diag = inertia + dep[1] / CELL_VOLUME + 2.0 * VISCOSITY
    known = [inertia * gas[c] + dep[2 + c] / CELL_VOLUME for c in range(3)]
    for s in range(CHUNKS):
        one = slice(s, s + 1)
        known_ref[s] = jnp.concatenate(
            [g[one] for g in gas] + [k[one] for k in known] + [diag[one], diag[one]], axis=0
        )
    low_ref[...] = known_ref[0]
    high_ref[...] = known_ref[CHUNKS - 1]


def sweeps_kernel(par_ref, near_ref, far_ref, known_ref, gas_out, table_ref):
    odd = par_ref[0] == 1
    below = jnp.where(odd, near_ref[...], far_ref[...])
    above = jnp.where(odd, far_ref[...], near_ref[...])
    full = jnp.concatenate([below] + [known_ref[s] for s in range(CHUNKS)] + [above], axis=1)
    width = full.shape[1]
    inverse = 1.0 / full[6:7]
    pad = jnp.zeros((5, width), F32)
    gas = jnp.concatenate([full[0:3], pad], axis=0)
    known = jnp.concatenate([full[3:6], pad], axis=0)
    for sweep in range(SWEEPS):
        sides = pltpu.roll(gas, 1, 1) + pltpu.roll(gas, width - 1, 1)
        gas = (known + VISCOSITY * sides) * inverse
    gas_out[...] = gas[0:3, BP : BP + CHUNKS * BP]
    for c in range(3):
        for s in range(CHUNKS):
            table_ref[c, s : s + 1, :] = gas[c : c + 1, (s + 1) * BP : (s + 2) * BP]


def pick_kernel(par_ref, owner_ref, cell_ref, mine_ref, other_ref, out_ref):
    par = par_ref[0]
    place_of = lax.broadcasted_iota(jnp.int32, (BP, BP), 0)
    quarter = lax.broadcasted_iota(jnp.int32, (CHUNKS, BP), 0)
    pad = jnp.zeros((4, BP), F32)
    for b in range(NB):
        cell = cell_ref[b : b + 1, :]
        chunk = cell // BP
        hot = jnp.where(place_of == cell % BP, 1.0, 0.0).astype(BF16)
        owner = owner_ref[b]
        chip = owner // 2
        mine = owner % 2 == par
        rows = [jnp.where(mine, mine_ref[chip, c], other_ref[chip, c]) for c in range(3)]
        rows = jnp.concatenate(rows + [pad], axis=0)
        stacked = jnp.concatenate(parts3(rows), axis=0).astype(BF16)
        found = jnp.dot(stacked, hot, preferred_element_type=F32)
        found = found[0:16] + found[16:32] + found[32:48]
        here = quarter == chunk
        out_ref[:, b * BP : (b + 1) * BP] = jnp.concatenate(
            [
                jnp.sum(jnp.where(here, found[4 * c : 4 * c + 4], 0.0), axis=0, keepdims=True)
                for c in range(3)
            ],
            axis=0,
        )


def swap_pairs(count):
    near = [(d, d ^ 1) for d in range(count)]
    far = [(d, (d + 1) % count if d % 2 else (d - 1) % count) for d in range(count)]
    return near, far


def body(
    positions,
    velocities,
    particle_volume,
    drag_coef,
    gas_at_particle,
    pair_first,
    pair_second,
    ghost_list,
    block_owner,
    cell_map,
    gas_velocity,
):
    axes = ("grp", "dom")
    ndom = lax.axis_size("dom")
    near_pairs, far_pairs = swap_pairs(lax.axis_size("grp") * ndom)

    def exchange(near, far):
        far = lax.ppermute(far, axes, far_pairs)
        near = lax.ppermute(near, axes, near_pairs)
        return near, far

    par = (lax.axis_index("dom") & 1).astype(jnp.int32).reshape(1)
    chips = ndom // 2
    same_core = [list(range(core, ndom, 2)) for core in range(2)]
    mass = particle_volume.reshape(NB, BP)
    beta = drag_coef.reshape(NB, BP)
    cells = cell_map.reshape(NB, BP)
    owner = block_owner.reshape(NB)

    state, aux, near, far, lists = prepare(
        par, ghost_list, positions, velocities, gas_at_particle, mass, beta, pair_first, pair_second
    )
    scalars = (par, ghost_list, lists, owner)
    rb = None
    for step in range(SUBSTEPS):
        near, far = exchange(near, far)
        part, g, rb = local_pairs(lists, state, rb)
        last = step == SUBSTEPS - 1
        outs = ghost_pairs(last, chips, scalars, cells, state, near, far, aux, part, g)
        if not last:
            state, near, far = outs
    pos_out, vel_out, keep, give = outs

    dep = keep + lax.ppermute(give, axes, near_pairs)
    dep = lax.all_to_all(dep, "dom", 0, 0, axis_index_groups=same_core, tiled=True)

    tile = jax.ShapeDtypeStruct((8, BP), F32)
    void, known, low, high = pl.pallas_call(
        known_kernel,
        in_specs=[VMEM] * 2,
        out_shape=(
            jax.ShapeDtypeStruct((CHUNKS, BP), F32),
            jax.ShapeDtypeStruct((CHUNKS, 8, BP), F32),
            tile,
            tile,
        ),
        out_specs=(VMEM,) * 4,
        compiler_params=PARAMS,
        cost_estimate=cost(400000, 700000),
        name="known",
    )(dep, gas_velocity)
    odd = par[0] == 1
    near, far = exchange(jnp.where(odd, low, high), jnp.where(odd, high, low))
    gas, table = pl.pallas_call(
        sweeps_kernel,
        in_specs=[SMEM] + [VMEM] * 3,
        out_shape=(
            jax.ShapeDtypeStruct((3, CHUNKS * BP), F32),
            jax.ShapeDtypeStruct((3, CHUNKS, BP), F32),
        ),
        out_specs=(VMEM,) * 2,
        compiler_params=PARAMS,
        cost_estimate=cost(40000, 50000),
        name="sweeps",
    )(par, near, far, known)

    table = jnp.broadcast_to(table[None], (chips, 3, CHUNKS, BP))
    table = lax.all_to_all(table, "dom", 0, 0, axis_index_groups=same_core, tiled=True)
    other = lax.ppermute(table, axes, near_pairs)
    particle_gas = pl.pallas_call(
        pick_kernel,
        in_specs=[SMEM] * 2 + [VMEM] * 3,
        out_shape=jax.ShapeDtypeStruct((3, NB * BP), F32),
        out_specs=VMEM,
        compiler_params=PARAMS,
        cost_estimate=cost(60000000, 900000),
        name="pick",
    )(par, owner, cells, table, other)
    return (pos_out, vel_out, gas, void.reshape(-1), particle_gas)


def solution(mesh):
    both = ("grp", "dom")
    return jax.shard_map(
        body,
        mesh=mesh,
        in_specs=(
            P(None, both),
            P(None, both),
            P(both),
            P(both),
            P(None, both),
            P(both),
            P(both),
            P(None, both),
            P(both, None),
            P(both),
            P(None, both),
        ),
        out_specs=(
            P(None, both),
            P(None, both),
            P(None, both),
            P(both),
            P(None, both),
        ),
        check_vma=False,
    )
```

```python
import functools

import jax
import jax.numpy as jnp
from jax import lax
from jax.experimental import pallas as pl
from jax.experimental.pallas import tpu as pltpu
from jax.sharding import PartitionSpec as P

NB = 32
BP = 128
NG = 2
NEXT = NB + 2 * NG
NPAIR = 128
GROUP = 8
SUBSTEPS = 4
SWEEPS = 4
K = 5
CHUNKS = 4
DEPROWS = 24
ROOM = NPAIR + 2 * GROUP
LISTS = 4 * ROOM + 8

SLAB = 4.0
SOFT = 0.01
STIFF = 20.0
STEP = 0.01
GRAVITY_Z = -1.0
RADIUS_FACTOR = 0.62
CELL_VOLUME = 16.0
RHO_STEP = 2.0
VISCOSITY = 1.0
TINY = 1e-36

F32 = jnp.float32
BF16 = jnp.bfloat16
VMEM = pl.BlockSpec(memory_space=pltpu.VMEM)
SMEM = pl.BlockSpec(memory_space=pltpu.SMEM)
PARAMS = pltpu.CompilerParams(vmem_limit_bytes=24 * 1024 * 1024)


def cost(flops, nbytes, transcendentals=0):
    return pl.CostEstimate(flops=flops, bytes_accessed=nbytes, transcendentals=transcendentals)


def parts3(value):
    high = value.astype(BF16).astype(F32)
    rest = value - high
    mid = rest.astype(BF16).astype(F32)
    low = (rest - mid).astype(BF16).astype(F32)
    return high, mid, low


def swap3(tile):
    return jnp.concatenate([tile[:, 3:6], tile[:, 0:3], tile[:, 6:8]], axis=1)


def fill_sends(par_ref, ghost_ref, state_ref, near_ref, far_ref):
    par = par_ref[0]
    for s in range(NG):
        near_ref[s] = state_ref[ghost_ref[par, s]]
        far_ref[s] = state_ref[ghost_ref[1 - par, s]]


def prepare_kernel(
    par_ref, ghost_hbm, pos_hbm, vel_hbm, gas_hbm, mass_hbm, beta_hbm, first_hbm, second_hbm,
    state_ref, aux_ref, near_ref, far_ref, list_ref,
    ghost_ref, pos_ref, vel_ref, gas_ref, mass_ref, beta_ref, first_ref, second_ref, sems,
):
    sources = (ghost_hbm, pos_hbm, vel_hbm, gas_hbm, mass_hbm, beta_hbm, first_hbm, second_hbm)
    targets = (ghost_ref, pos_ref, vel_ref, gas_ref, mass_ref, beta_ref, first_ref, second_ref)
    copies = [pltpu.make_async_copy(s, t, sems.at[i]) for i, (s, t) in enumerate(zip(sources, targets))]
    for copy in copies:
        copy.start()
    for copy in copies:
        copy.wait()
    radius = RADIUS_FACTOR * jnp.exp(jnp.log(mass_ref[...]) * (1.0 / 3.0))
    zero3 = jnp.zeros((3, BP), F32)
    for b in range(NB):
        lanes = slice(b * BP, (b + 1) * BP)
        rows = slice(b, b + 1)
        state_ref[b] = jnp.concatenate(
            [pos_ref[:, lanes], vel_ref[:, lanes], radius[rows], jnp.zeros((1, BP), F32)], axis=0
        )
        aux_ref[b] = jnp.concatenate([zero3, gas_ref[:, lanes], beta_ref[rows], mass_ref[rows]], axis=0)
    fill_sends(par_ref, ghost_ref, state_ref, near_ref, far_ref)

    def sort_pair(p, counts):
        local, ghost = counts
        first = first_ref[p]
        second = second_ref[p]
        is_ghost = (second >= NB).astype(jnp.int32)
        slot = jnp.where(is_ghost == 1, 2 * ROOM + ghost, GROUP + local)
        list_ref[slot] = first
        list_ref[ROOM + slot] = second
        return local + 1 - is_ghost, ghost + is_ghost

    local, ghost = lax.fori_loop(0, NPAIR, sort_pair, (jnp.int32(0), jnp.int32(0)))
    for s in range(GROUP):
        list_ref[s] = NB
        list_ref[ROOM + s] = 0
        list_ref[GROUP + local + s] = NB
        list_ref[ROOM + GROUP + local + s] = 0
        list_ref[2 * ROOM + ghost + s] = NB
        list_ref[3 * ROOM + ghost + s] = NB
    list_ref[4 * ROOM] = (local + GROUP - 1) // GROUP
    list_ref[4 * ROOM + 1] = (ghost + GROUP - 1) // GROUP


def prepare(par, ghost_list, pos, vel, gas_seen, mass, beta, first, second):
    tile = jax.ShapeDtypeStruct((NB, 8, BP), F32)
    send = jax.ShapeDtypeStruct((NG, 8, BP), F32)
    lists = jax.ShapeDtypeStruct((LISTS,), jnp.int32)
    return pl.pallas_call(
        prepare_kernel,
        in_specs=[SMEM] + [pl.BlockSpec(memory_space=pl.ANY)] * 8,
        out_shape=(tile, tile, send, send, lists),
        out_specs=(VMEM,) * 4 + (SMEM,),
        scratch_shapes=[
            pltpu.SMEM((2, NG), jnp.int32),
            pltpu.VMEM((3, NB * BP), F32),
            pltpu.VMEM((3, NB * BP), F32),
            pltpu.VMEM((3, NB * BP), F32),
            pltpu.VMEM((NB, BP), F32),
            pltpu.VMEM((NB, BP), F32),
            pltpu.SMEM((NPAIR,), jnp.int32),
            pltpu.SMEM((NPAIR,), jnp.int32),
            pltpu.SemaphoreType.DMA((8,)),
        ],
        compiler_params=pltpu.CompilerParams(vmem_limit_bytes=58 * 1024 * 1024),
        cost_estimate=cost(100000, 600000),
        name="prepare",
    )(par, ghost_list, pos, vel, gas_seen, mass, beta, first, second)


def row_index():
    return lax.broadcasted_iota(jnp.int32, (8, BP), 0)[None]


def features(tile):
    row = row_index()
    swapped = swap3(tile)
    norm = jnp.sum(jnp.where(row < 3, tile * tile, 0.0), axis=1, keepdims=True)
    cross = jnp.sum(jnp.where(row < 3, tile * swapped, 0.0), axis=1, keepdims=True) * (1.0 / STIFF)
    return swapped, norm, cross


def partner_side(tile, base, jt_ref, a_ref):
    row = row_index()
    ones = jnp.ones((8, BP), F32)
    zeros = jnp.zeros((8, BP), F32)
    swapped, norm, cross = features(tile)
    full = jnp.where(row < 6, tile, jnp.where(row == 6, norm, cross))
    high, mid, low = parts3(full)
    for s in range(tile.shape[0]):
        h, m, l = high[s], mid[s], low[s]
        stack = jnp.concatenate([h, h, h, m, m, l, ones, zeros], axis=0)
        jt_ref[base + s] = jnp.transpose(stack).astype(BF16)
        tail = [ones[0:1], zeros[0:6]]
        by_x = jnp.concatenate([h[0:3], m[0:3], l[0:3]] + tail, axis=0)
        by_v = jnp.concatenate([h[3:6], m[3:6], l[3:6]] + tail, axis=0)
        a_ref[base + s] = jnp.concatenate([by_x, by_v], axis=1).astype(BF16)


def own_side(tile, base, g_ref):
    row = row_index()
    zeros = jnp.zeros((8, BP), F32)
    swapped, norm, cross = features(tile)
    xh, xm, xl = parts3(jnp.where(row < 3, -2.0 * tile, 0.0))
    xh = jnp.where(row == 6, 1.0, xh)
    vh, vm, vl = parts3(jnp.where(row < 6, swapped * (-1.0 / STIFF), 0.0))
    vh = jnp.where(row == 7, 1.0, vh)
    nh, nm, nl = parts3(norm + SOFT)
    ch, cm, cl = parts3(cross)
    own_n = jnp.where(row == 0, nh, jnp.where(row == 1, nm, jnp.where(row == 2, nl, 0.0)))
    own_c = jnp.where(row == 0, ch, jnp.where(row == 1, cm, jnp.where(row == 2, cl, 0.0)))
    for s in range(tile.shape[0]):
        left = jnp.concatenate([xh[s], xm[s], xl[s], xh[s], xm[s], xh[s], own_n[s], zeros], axis=0)
        right = jnp.concatenate([vh[s], vm[s], vl[s], vh[s], vm[s], vh[s], own_c[s], zeros], axis=0)
        g_ref[base + s] = jnp.concatenate([left, right], axis=1).astype(BF16)


def pair_product(a, b, jt_ref, g_ref):
    return jnp.dot(jt_ref[b], g_ref[a], preferred_element_type=F32)


def pair_weights(both, a, b, state_ref, rb_ref):
    dist2 = both[:, :BP]
    slide = both[:, BP:]
    inv = lax.rsqrt(dist2)
    overlap = (rb_ref[b] + state_ref[a, 6:7, :]) - dist2 * inv
    delta = jnp.maximum(overlap, 0.0)
    root = delta * lax.rsqrt(jnp.maximum(overlap, TINY))
    push = (root * inv) * (delta - slide * inv)
    push_high = push.astype(BF16)
    push_low = (push - push_high.astype(F32)).astype(BF16)
    root_high = root.astype(BF16)
    root_low = (root - root_high.astype(F32)).astype(BF16)
    return jnp.concatenate([push_high, push_low, root_high, root_low], axis=0)


def partner_sums(b, weights, a_ref):
    left_x = a_ref[b, :, :BP]
    left_v = a_ref[b, :, BP:]
    left_x = jnp.concatenate([left_x, left_x], axis=1)
    left_v = jnp.concatenate([left_v, left_v], axis=1)
    by_x = jnp.dot(left_x, weights[: 2 * BP], preferred_element_type=F32)
    by_v = jnp.dot(left_v, weights[2 * BP :], preferred_element_type=F32)
    return jnp.concatenate([by_x, by_v], axis=0)


def ghost_loop(groups, list_ref, acc_ref, state_ref, jt_ref, g_ref, a_ref, rb_ref):
    def group(k, carry):
        start = 2 * ROOM + k * GROUP
        firsts = [list_ref[start + s] for s in range(GROUP)]
        sums = []
        for s in range(GROUP):
            a = jnp.minimum(firsts[s], NB - 1)
            b = list_ref[start + ROOM + s] - NB
            weights = pair_weights(pair_product(a, b, jt_ref, g_ref), a, b, state_ref, rb_ref)
            sums.append(partner_sums(b, weights, a_ref))
        for a, value in zip(firsts, sums):
            acc_ref[a] += value
        return carry

    lax.fori_loop(0, groups, group, 0)


def local_loop(groups, list_ref, acc_ref, state_ref, jt_ref, g_ref, a_ref, rb_ref, held_ref):
    def finish(start, s):
        a = list_ref[start + s]
        b = list_ref[ROOM + start + s]
        acc_ref[a] += partner_sums(b, held_ref[s], a_ref)

    def group(k, carry):
        start = k * GROUP
        for s in range(GROUP):
            a = jnp.minimum(list_ref[start + GROUP + s], NB - 1)
            b = list_ref[ROOM + start + GROUP + s]
            both = pair_product(a, b, jt_ref, g_ref)
            finish(start, s)
            held_ref[s] = pair_weights(both, a, b, state_ref, rb_ref)
        return carry

    held_ref[...] = jnp.zeros(held_ref.shape, BF16)
    lax.fori_loop(0, groups, group, 0)
    for s in range(GROUP):
        finish(groups * GROUP, s)


def local_kernel(opening, *refs):
    if opening:
        list_ref, state_ref, acc_ref, g_ref, rb_ref, jt_ref, a_ref, held_ref = refs
        column = jnp.transpose(state_ref[:, 6, :])
        for b in range(NB):
            rb_ref[b] = jnp.broadcast_to(column[:, b : b + 1], (BP, BP))
    else:
        list_ref, state_ref, rb_ref, acc_ref, g_ref, jt_ref, a_ref, held_ref = refs

    def blocks(k, carry):
        tile = state_ref[pl.ds(k * 8, 8)]
        partner_side(tile, k * 8, jt_ref, a_ref)
        own_side(tile, k * 8, g_ref)
        return carry

    lax.fori_loop(0, NB // 8, blocks, 0)
    acc_ref[...] = jnp.zeros(acc_ref.shape, F32)
    local_loop(list_ref[4 * ROOM], list_ref, acc_ref, state_ref, jt_ref, g_ref, a_ref, rb_ref, held_ref)


def local_pairs(lists, state, rb=None):
    opening = rb is None
    outs = (
        jax.ShapeDtypeStruct((NB + 1, 32, BP), F32),
        jax.ShapeDtypeStruct((NB, 64, 2 * BP), BF16),
    )
    wide = (jax.ShapeDtypeStruct((NB, BP, BP), F32),)
    args = (lists, state) if opening else (lists, state, rb)
    outs = pl.pallas_call(
        functools.partial(local_kernel, opening),
        in_specs=[SMEM] + [VMEM] * (len(args) - 1),
        out_shape=outs + (wide if opening else ()),
        out_specs=(VMEM,) * (3 if opening else 2),
        scratch_shapes=[
            pltpu.VMEM((NB, BP, 64), BF16),
            pltpu.VMEM((NB, 16, 2 * BP), BF16),
            pltpu.VMEM((GROUP, 4 * BP, BP), BF16),
        ],
        compiler_params=PARAMS,
        cost_estimate=cost(10000000000, 3500000, 4000000),
        name="local_pairs",
    )(*args)
    return outs if opening else (*outs, rb)


def ghost_kernel(last, *refs):
    (par_ref, ghost_ref, list_ref, owner_ref), refs = refs[:4], refs[4:]
    (cell_ref, state_ref, near_in, far_in, aux_ref, part_ref, g_ref), refs = refs[:7], refs[7:]
    if last:
        (pos_out, vel_out, keep_ref, give_ref), (*scratch, spread_ref) = refs[:4], refs[4:]
    else:
        (new_ref, near_out, far_out), scratch = refs[:3], refs[3:]
    ext_ref, jt_ref, a_ref, rb_ref, acc_ref = scratch
    par = par_ref[0]
    row = row_index()

    sign = 1.0 - 2.0 * par.astype(F32)
    shift = jnp.where(row[0] == 0, SLAB * sign, 0.0)
    for s in range(NG):
        ext_ref[NG * (1 - par) + s] = near_in[s] + shift
        ext_ref[NG * par + s] = far_in[s] - shift
    for s in range(2 * NG, 8):
        ext_ref[s] = jnp.zeros((8, BP), F32)
    column = jnp.transpose(ext_ref[:, 6, :])
    for b in range(2 * NG):
        rb_ref[b] = jnp.broadcast_to(column[:, b : b + 1], (BP, BP))
    partner_side(ext_ref[0:4], 0, jt_ref, a_ref)
    acc_ref[...] = part_ref[...]
    ghost_loop(list_ref[4 * ROOM + 1], list_ref, acc_ref, state_ref, jt_ref, g_ref, a_ref, rb_ref)

    tile = state_ref[...]
    raw = acc_ref[0:NB]
    acc = jnp.concatenate(
        [
            raw[:, 0:3] + raw[:, 3:6] + raw[:, 6:9],
            raw[:, 16:19] + raw[:, 19:22] + raw[:, 22:25],
            raw[:, 9:10],
            raw[:, 25:26],
        ],
        axis=1,
    )
    aux = aux_ref[...]
    by_x = STIFF * (tile * acc[:, 6:7] - acc)
    by_v = acc - tile * acc[:, 7:8]
    force = swap3(by_x) + by_v
    beta = aux[:, 6:7]
    mass = aux[:, 7:8]
    gravity = jnp.where(row == 5, GRAVITY_Z, 0.0)
    velocity = tile + STEP * ((force + beta * (aux - tile)) / mass + gravity)
    place = tile + STEP * swap3(velocity)
    moved = jnp.where(row < 3, place, jnp.where(row < 6, velocity, tile))

    if not last:
        new_ref[...] = moved
        fill_sends(par_ref, ghost_ref, new_ref, near_out, far_out)
        return

    for b in range(NB):
        lanes = slice(b * BP, (b + 1) * BP)
        pos_out[:, lanes] = moved[b, 0:3]
        vel_out[:, lanes] = moved[b, 3:6]

    keep_ref[...] = jnp.zeros(keep_ref.shape, F32)
    give_ref[...] = jnp.zeros(give_ref.shape, F32)
    drag = beta * moved
    quarter = lax.broadcasted_iota(jnp.int32, (DEPROWS, BP), 0) % CHUNKS
    place_of = lax.broadcasted_iota(jnp.int32, (BP, BP), 0)
    zeros = jnp.zeros((8, BP), F32)
    tail = jnp.zeros((DEPROWS - CHUNKS * K, BP), F32)
    for b in range(NB):
        cell = cell_ref[b : b + 1, :]
        chunk = cell // BP
        hot = jnp.where(place_of == cell % BP, 1.0, 0.0).astype(BF16)
        values = [mass[b], beta[b], drag[b, 3:4], drag[b, 4:5], drag[b, 5:6]]
        amounts = jnp.concatenate([jnp.broadcast_to(v, (CHUNKS, BP)) for v in values] + [tail], axis=0)
        amounts = jnp.where(quarter == chunk, amounts, 0.0)
        stacked = jnp.concatenate(list(parts3(amounts)) + [zeros], axis=0).astype(BF16)
        spread = lax.dot_general(stacked, hot, (((1,), (1,)), ((), ())), preferred_element_type=F32)
        spread_ref[b] = spread[0:DEPROWS] + spread[DEPROWS : 2 * DEPROWS] + spread[2 * DEPROWS : 3 * DEPROWS]

    for b in range(NB):
        owner = owner_ref[b]

        def put(target, b=b, chip=owner // 2):
            for q in range(K):
                target[chip, q] += spread_ref[b, CHUNKS * q : CHUNKS * (q + 1)]

        mine = owner % 2 == par
        pl.when(mine)(functools.partial(put, keep_ref))
        pl.when(jnp.logical_not(mine))(functools.partial(put, give_ref))


def ghost_pairs(last, chips, scalars, cells, state, near, far, aux, part, g):
    tile = jax.ShapeDtypeStruct((NB, 8, BP), F32)
    send = jax.ShapeDtypeStruct((NG, 8, BP), F32)
    if last:
        flat = jax.ShapeDtypeStruct((3, NB * BP), F32)
        dep = jax.ShapeDtypeStruct((chips, K, CHUNKS, BP), F32)
        outs = (flat, flat, dep, dep)
    else:
        outs = (tile, send, send)
    return pl.pallas_call(
        functools.partial(ghost_kernel, last),
        in_specs=[SMEM] * 4 + [VMEM] * 7,
        out_shape=outs,
        out_specs=(VMEM,) * len(outs),
        scratch_shapes=[
            pltpu.VMEM((8, 8, BP), F32),
            pltpu.VMEM((2 * NG, BP, 64), BF16),
            pltpu.VMEM((2 * NG, 16, 2 * BP), BF16),
            pltpu.VMEM((2 * NG, BP, BP), F32),
            pltpu.VMEM((NB + 1, 32, BP), F32),
        ]
        + ([pltpu.VMEM((NB, DEPROWS, BP), F32)] if last else []),
        compiler_params=PARAMS,
        cost_estimate=cost(2000000000, 2000000, 500000),
        name="ghost_pairs_last" if last else "ghost_pairs",
    )(*scalars, cells, state, near, far, aux, part, g)


def known_kernel(dep_ref, gas_ref, void_ref, known_ref, low_ref, high_ref):
    dep = jnp.sum(dep_ref[...], axis=0)
    void = CELL_VOLUME / (CELL_VOLUME + dep[0])
    inertia = RHO_STEP * void
    void_ref[...] = void
    gas = [
        jnp.concatenate([gas_ref[c : c + 1, s * BP : (s + 1) * BP] for s in range(CHUNKS)], axis=0)
        for c in range(3)
    ]
    diag = inertia + dep[1] / CELL_VOLUME + 2.0 * VISCOSITY
    known = [inertia * gas[c] + dep[2 + c] / CELL_VOLUME for c in range(3)]
    for s in range(CHUNKS):
        one = slice(s, s + 1)
        known_ref[s] = jnp.concatenate(
            [g[one] for g in gas] + [k[one] for k in known] + [diag[one], diag[one]], axis=0
        )
    low_ref[...] = known_ref[0]
    high_ref[...] = known_ref[CHUNKS - 1]


def sweeps_kernel(par_ref, near_ref, far_ref, known_ref, gas_out, table_ref):
    odd = par_ref[0] == 1
    below = jnp.where(odd, near_ref[...], far_ref[...])
    above = jnp.where(odd, far_ref[...], near_ref[...])
    full = jnp.concatenate([below] + [known_ref[s] for s in range(CHUNKS)] + [above], axis=1)
    width = full.shape[1]
    inverse = 1.0 / full[6:7]
    pad = jnp.zeros((5, width), F32)
    gas = jnp.concatenate([full[0:3], pad], axis=0)
    known = jnp.concatenate([full[3:6], pad], axis=0)
    for sweep in range(SWEEPS):
        sides = pltpu.roll(gas, 1, 1) + pltpu.roll(gas, width - 1, 1)
        gas = (known + VISCOSITY * sides) * inverse
    gas_out[...] = gas[0:3, BP : BP + CHUNKS * BP]
    for c in range(3):
        for s in range(CHUNKS):
            table_ref[c, s : s + 1, :] = gas[c : c + 1, (s + 1) * BP : (s + 2) * BP]


def pick_kernel(par_ref, owner_ref, cell_ref, mine_ref, other_ref, out_ref):
    par = par_ref[0]
    place_of = lax.broadcasted_iota(jnp.int32, (BP, BP), 0)
    quarter = lax.broadcasted_iota(jnp.int32, (CHUNKS, BP), 0)
    pad = jnp.zeros((4, BP), F32)
    for b in range(NB):
        cell = cell_ref[b : b + 1, :]
        chunk = cell // BP
        hot = jnp.where(place_of == cell % BP, 1.0, 0.0).astype(BF16)
        owner = owner_ref[b]
        chip = owner // 2
        mine = owner % 2 == par
        rows = [jnp.where(mine, mine_ref[chip, c], other_ref[chip, c]) for c in range(3)]
        rows = jnp.concatenate(rows + [pad], axis=0)
        stacked = jnp.concatenate(parts3(rows), axis=0).astype(BF16)
        found = jnp.dot(stacked, hot, preferred_element_type=F32)
        found = found[0:16] + found[16:32] + found[32:48]
        here = quarter == chunk
        out_ref[:, b * BP : (b + 1) * BP] = jnp.concatenate(
            [
                jnp.sum(jnp.where(here, found[4 * c : 4 * c + 4], 0.0), axis=0, keepdims=True)
                for c in range(3)
            ],
            axis=0,
        )


def swap_pairs(count):
    near = [(d, d ^ 1) for d in range(count)]
    far = [(d, (d + 1) % count if d % 2 else (d - 1) % count) for d in range(count)]
    return near, far


def body(
    positions,
    velocities,
    particle_volume,
    drag_coef,
    gas_at_particle,
    pair_first,
    pair_second,
    ghost_list,
    block_owner,
    cell_map,
    gas_velocity,
):
    axes = ("grp", "dom")
    ndom = lax.axis_size("dom")
    near_pairs, far_pairs = swap_pairs(lax.axis_size("grp") * ndom)

    def exchange(near, far):
        far = lax.ppermute(far, axes, far_pairs)
        near = lax.ppermute(near, axes, near_pairs)
        return near, far

    par = (lax.axis_index("dom") & 1).astype(jnp.int32).reshape(1)
    chips = ndom // 2
    same_core = [list(range(core, ndom, 2)) for core in range(2)]
    mass = particle_volume.reshape(NB, BP)
    beta = drag_coef.reshape(NB, BP)
    cells = cell_map.reshape(NB, BP)
    owner = block_owner.reshape(NB)

    state, aux, near, far, lists = prepare(
        par, ghost_list, positions, velocities, gas_at_particle, mass, beta, pair_first, pair_second
    )
    scalars = (par, ghost_list, lists, owner)
    rb = None
    for step in range(SUBSTEPS):
        near, far = exchange(near, far)
        part, g, rb = local_pairs(lists, state, rb)
        last = step == SUBSTEPS - 1
        outs = ghost_pairs(last, chips, scalars, cells, state, near, far, aux, part, g)
        if not last:
            state, near, far = outs
    pos_out, vel_out, keep, give = outs

    dep = keep + lax.ppermute(give, axes, near_pairs)
    dep = lax.all_to_all(dep, "dom", 0, 0, axis_index_groups=same_core, tiled=True)

    tile = jax.ShapeDtypeStruct((8, BP), F32)
    void, known, low, high = pl.pallas_call(
        known_kernel,
        in_specs=[VMEM] * 2,
        out_shape=(
            jax.ShapeDtypeStruct((CHUNKS, BP), F32),
            jax.ShapeDtypeStruct((CHUNKS, 8, BP), F32),
            tile,
            tile,
        ),
        out_specs=(VMEM,) * 4,
        compiler_params=PARAMS,
        cost_estimate=cost(400000, 700000),
        name="known",
    )(dep, gas_velocity)
    odd = par[0] == 1
    near, far = exchange(jnp.where(odd, low, high), jnp.where(odd, high, low))
    gas, table = pl.pallas_call(
        sweeps_kernel,
        in_specs=[SMEM] + [VMEM] * 3,
        out_shape=(
            jax.ShapeDtypeStruct((3, CHUNKS * BP), F32),
            jax.ShapeDtypeStruct((3, CHUNKS, BP), F32),
        ),
        out_specs=(VMEM,) * 2,
        compiler_params=PARAMS,
        cost_estimate=cost(40000, 50000),
        name="sweeps",
    )(par, near, far, known)

    table = jnp.broadcast_to(table[None], (chips, 3, CHUNKS, BP))
    table = lax.all_to_all(table, "dom", 0, 0, axis_index_groups=same_core, tiled=True)
    other = lax.ppermute(table, axes, near_pairs)
    particle_gas = pl.pallas_call(
        pick_kernel,
        in_specs=[SMEM] * 2 + [VMEM] * 3,
        out_shape=jax.ShapeDtypeStruct((3, NB * BP), F32),
        out_specs=VMEM,
        compiler_params=PARAMS,
        cost_estimate=cost(60000000, 900000),
        name="pick",
    )(par, owner, cells, table, other)
    return (pos_out, vel_out, gas, void.reshape(-1), particle_gas)


def solution(mesh):
    both = ("grp", "dom")
    return jax.shard_map(
        body,
        mesh=mesh,
        in_specs=(
            P(None, both),
            P(None, both),
            P(both),
            P(both),
            P(None, both),
            P(both),
            P(both),
            P(None, both),
            P(both, None),
            P(both),
            P(None, both),
        ),
        out_specs=(
            P(None, both),
            P(None, both),
            P(None, both),
            P(both),
            P(None, both),
        ),
        check_vma=False,
    )
```

```python
import functools

import jax
import jax.numpy as jnp
from jax import lax
from jax.experimental import pallas as pl
from jax.experimental.pallas import tpu as pltpu
from jax.sharding import PartitionSpec as P

NB = 32
BP = 128
NG = 2
NEXT = NB + 2 * NG
NPAIR = 128
GROUP = 8
SUBSTEPS = 4
SWEEPS = 4
K = 5
CHUNKS = 4
DEPROWS = 24
DEPTH = 48
ROOM = NPAIR + 2 * GROUP
LISTS = 4 * ROOM + 8

SLAB = 4.0
SOFT = 0.01
STIFF = 20.0
STEP = 0.01
GRAVITY_Z = -1.0
RADIUS_FACTOR = 0.62
CELL_VOLUME = 16.0
RHO_STEP = 2.0
VISCOSITY = 1.0
TINY = 1e-36

F32 = jnp.float32
BF16 = jnp.bfloat16
VMEM = pl.BlockSpec(memory_space=pltpu.VMEM)
SMEM = pl.BlockSpec(memory_space=pltpu.SMEM)
PARAMS = pltpu.CompilerParams(vmem_limit_bytes=24 * 1024 * 1024)


def cost(flops, nbytes, transcendentals=0):
    return pl.CostEstimate(flops=flops, bytes_accessed=nbytes, transcendentals=transcendentals)


def parts3(value):
    high = value.astype(BF16).astype(F32)
    rest = value - high
    mid = rest.astype(BF16).astype(F32)
    low = (rest - mid).astype(BF16).astype(F32)
    return high, mid, low


def swap3(tile):
    return jnp.concatenate([tile[:, 3:6], tile[:, 0:3], tile[:, 6:8]], axis=1)


def fill_sends(par_ref, ghost_ref, state_ref, near_ref, far_ref):
    par = par_ref[0]
    for s in range(NG):
        near_ref[s] = state_ref[ghost_ref[par, s]]
        far_ref[s] = state_ref[ghost_ref[1 - par, s]]


def prepare_kernel(
    par_ref, ghost_hbm, pos_hbm, vel_hbm, gas_hbm, mass_hbm, beta_hbm, first_hbm, second_hbm,
    state_ref, aux_ref, near_ref, far_ref, list_ref,
    ghost_ref, pos_ref, vel_ref, gas_ref, mass_ref, beta_ref, first_ref, second_ref, sems,
):
    sources = (ghost_hbm, pos_hbm, vel_hbm, gas_hbm, mass_hbm, beta_hbm, first_hbm, second_hbm)
    targets = (ghost_ref, pos_ref, vel_ref, gas_ref, mass_ref, beta_ref, first_ref, second_ref)
    copies = [pltpu.make_async_copy(s, t, sems.at[i]) for i, (s, t) in enumerate(zip(sources, targets))]
    for copy in copies:
        copy.start()
    for copy in copies:
        copy.wait()
    radius = RADIUS_FACTOR * jnp.exp(jnp.log(mass_ref[...]) * (1.0 / 3.0))
    zero3 = jnp.zeros((3, BP), F32)
    for b in range(NB):
        lanes = slice(b * BP, (b + 1) * BP)
        rows = slice(b, b + 1)
        state_ref[b] = jnp.concatenate(
            [pos_ref[:, lanes], vel_ref[:, lanes], radius[rows], jnp.zeros((1, BP), F32)], axis=0
        )
        aux_ref[b] = jnp.concatenate([zero3, gas_ref[:, lanes], beta_ref[rows], mass_ref[rows]], axis=0)
    fill_sends(par_ref, ghost_ref, state_ref, near_ref, far_ref)

    def sort_pair(p, counts):
        local, ghost = counts
        first = first_ref[p]
        second = second_ref[p]
        is_ghost = (second >= NB).astype(jnp.int32)
        slot = jnp.where(is_ghost == 1, 2 * ROOM + ghost, GROUP + local)
        list_ref[slot] = first
        list_ref[ROOM + slot] = second
        return local + 1 - is_ghost, ghost + is_ghost

    local, ghost = lax.fori_loop(0, NPAIR, sort_pair, (jnp.int32(0), jnp.int32(0)), unroll=4)
    for s in range(GROUP):
        list_ref[s] = NB
        list_ref[ROOM + s] = 0
        list_ref[GROUP + local + s] = NB
        list_ref[ROOM + GROUP + local + s] = 0
        list_ref[2 * ROOM + ghost + s] = NB
        list_ref[3 * ROOM + ghost + s] = NB
    list_ref[4 * ROOM] = (local + GROUP - 1) // GROUP
    list_ref[4 * ROOM + 1] = (ghost + GROUP - 1) // GROUP


def prepare(par, ghost_list, pos, vel, gas_seen, mass, beta, first, second):
    tile = jax.ShapeDtypeStruct((NB, 8, BP), F32)
    send = jax.ShapeDtypeStruct((NG, 8, BP), F32)
    lists = jax.ShapeDtypeStruct((LISTS,), jnp.int32)
    return pl.pallas_call(
        prepare_kernel,
        in_specs=[SMEM] + [pl.BlockSpec(memory_space=pl.ANY)] * 8,
        out_shape=(tile, tile, send, send, lists),
        out_specs=(VMEM,) * 4 + (SMEM,),
        scratch_shapes=[
            pltpu.SMEM((2, NG), jnp.int32),
            pltpu.VMEM((3, NB * BP), F32),
            pltpu.VMEM((3, NB * BP), F32),
            pltpu.VMEM((3, NB * BP), F32),
            pltpu.VMEM((NB, BP), F32),
            pltpu.VMEM((NB, BP), F32),
            pltpu.SMEM((NPAIR,), jnp.int32),
            pltpu.SMEM((NPAIR,), jnp.int32),
            pltpu.SemaphoreType.DMA((8,)),
        ],
        compiler_params=pltpu.CompilerParams(vmem_limit_bytes=58 * 1024 * 1024),
        cost_estimate=cost(100000, 600000),
        name="prepare",
    )(par, ghost_list, pos, vel, gas_seen, mass, beta, first, second)


def row_index():
    return lax.broadcasted_iota(jnp.int32, (8, BP), 0)[None]


def features(tile):
    row = row_index()
    swapped = swap3(tile)
    norm = jnp.sum(jnp.where(row < 3, tile * tile, 0.0), axis=1, keepdims=True)
    cross = jnp.sum(jnp.where(row < 3, tile * swapped, 0.0), axis=1, keepdims=True) * (1.0 / STIFF)
    return swapped, norm, cross


def partner_side(tile, base, jt_ref, a_ref):
    row = row_index()
    ones = jnp.ones((8, BP), F32)
    zeros = jnp.zeros((8, BP), F32)
    swapped, norm, cross = features(tile)
    full = jnp.where(row < 6, tile, jnp.where(row == 6, norm, cross))
    high, mid, low = parts3(full)
    for s in range(tile.shape[0]):
        h, m, l = high[s], mid[s], low[s]
        h_one = jnp.where(row[0] < 6, h, 1.0)
        m_one = jnp.where(row[0] < 6, m, 1.0)
        stack = jnp.concatenate([h, h_one, h_one, m, m_one, l], axis=0)
        jt_ref[base + s] = jnp.transpose(stack).astype(BF16)
        tail = [ones[0:1], zeros[0:6]]
        by_x = jnp.concatenate([h[0:3], m[0:3], l[0:3]] + tail, axis=0)
        by_v = jnp.concatenate([h[3:6], m[3:6], l[3:6]] + tail, axis=0)
        a_ref[base + s] = jnp.concatenate([by_x, by_v], axis=1).astype(BF16)


def own_side(tile, base, g_ref):
    row = row_index()
    swapped, norm, cross = features(tile)
    xh, xm, xl = parts3(jnp.where(row < 3, -2.0 * tile, 0.0))
    xh = jnp.where(row == 6, 1.0, xh)
    vh, vm, vl = parts3(jnp.where(row < 6, swapped * (-1.0 / STIFF), 0.0))
    vh = jnp.where(row == 7, 1.0, vh)
    nh, nm, nl = parts3(norm + SOFT)
    ch, cm, cl = parts3(cross)
    lefts = (xh, jnp.where(row == 6, nh, xm), jnp.where(row == 6, nm, xl), xh, jnp.where(row == 6, nl, xm), xh)
    rights = (vh, jnp.where(row == 7, ch, vm), jnp.where(row == 7, cm, vl), vh, jnp.where(row == 7, cl, vm), vh)
    for s in range(tile.shape[0]):
        left = jnp.concatenate([part[s] for part in lefts], axis=0)
        right = jnp.concatenate([part[s] for part in rights], axis=0)
        g_ref[base + s] = jnp.concatenate([left, right], axis=1).astype(BF16)


def pair_product(a, b, jt_ref, g_ref):
    return jnp.dot(jt_ref[b], g_ref[a], preferred_element_type=F32)


def pair_weights(both, a, b, state_ref, rb_ref):
    dist2 = both[:, :BP]
    slide = both[:, BP:]
    inv = lax.rsqrt(dist2)
    overlap = (rb_ref[b] + state_ref[a, 6:7, :]) - dist2 * inv
    delta = jnp.maximum(overlap, 0.0)
    root = delta * lax.rsqrt(jnp.maximum(overlap, TINY))
    push = (root * inv) * (delta - slide * inv)
    push_high = push.astype(BF16)
    push_low = (push - push_high.astype(F32)).astype(BF16)
    root_high = root.astype(BF16)
    root_low = (root - root_high.astype(F32)).astype(BF16)
    return jnp.concatenate([push_high, push_low, root_high, root_low], axis=0)


def partner_sums(b, weights, a_ref):
    left_x = a_ref[b, :, :BP]
    left_v = a_ref[b, :, BP:]
    left_x = jnp.concatenate([left_x, left_x], axis=1)
    left_v = jnp.concatenate([left_v, left_v], axis=1)
    by_x = jnp.dot(left_x, weights[: 2 * BP], preferred_element_type=F32)
    by_v = jnp.dot(left_v, weights[2 * BP :], preferred_element_type=F32)
    return jnp.concatenate([by_x, by_v], axis=0)


def ghost_loop(groups, list_ref, acc_ref, state_ref, jt_ref, g_ref, a_ref, rb_ref):
    def group(k, carry):
        start = 2 * ROOM + k * GROUP
        firsts = [list_ref[start + s] for s in range(GROUP)]
        sums = []
        for s in range(GROUP):
            a = jnp.minimum(firsts[s], NB - 1)
            b = list_ref[start + ROOM + s] - NB
            weights = pair_weights(pair_product(a, b, jt_ref, g_ref), a, b, state_ref, rb_ref)
            sums.append(partner_sums(b, weights, a_ref))
        for a, value in zip(firsts, sums):
            acc_ref[a] += value
        return carry

    lax.fori_loop(0, groups, group, 0)


def local_loop(groups, list_ref, acc_ref, state_ref, jt_ref, g_ref, a_ref, rb_ref, held_ref):
    def finish(start, s):
        a = list_ref[start + s]
        b = list_ref[ROOM + start + s]
        acc_ref[a] += partner_sums(b, held_ref[s], a_ref)

    def group(k, carry):
        start = k * GROUP
        for s in range(GROUP):
            a = jnp.minimum(list_ref[start + GROUP + s], NB - 1)
            b = list_ref[ROOM + start + GROUP + s]
            both = pair_product(a, b, jt_ref, g_ref)
            finish(start, s)
            held_ref[s] = pair_weights(both, a, b, state_ref, rb_ref)
        return carry

    held_ref[...] = jnp.zeros(held_ref.shape, BF16)
    lax.fori_loop(0, groups, group, 0)
    for s in range(GROUP):
        finish(groups * GROUP, s)


def local_kernel(opening, *refs):
    if opening:
        list_ref, state_ref, acc_ref, g_ref, rb_ref, jt_ref, a_ref, held_ref = refs
        column = jnp.transpose(state_ref[:, 6, :])
        for b in range(NB):
            rb_ref[b] = jnp.broadcast_to(column[:, b : b + 1], (BP, BP))
    else:
        list_ref, state_ref, rb_ref, acc_ref, g_ref, jt_ref, a_ref, held_ref = refs

    def blocks(k, carry):
        tile = state_ref[pl.ds(k * 8, 8)]
        partner_side(tile, k * 8, jt_ref, a_ref)
        own_side(tile, k * 8, g_ref)
        return carry

    lax.fori_loop(0, NB // 8, blocks, 0)
    acc_ref[...] = jnp.zeros(acc_ref.shape, F32)
    local_loop(list_ref[4 * ROOM], list_ref, acc_ref, state_ref, jt_ref, g_ref, a_ref, rb_ref, held_ref)


def local_pairs(lists, state, rb=None):
    opening = rb is None
    outs = (
        jax.ShapeDtypeStruct((NB + 1, 32, BP), F32),
        jax.ShapeDtypeStruct((NB, DEPTH, 2 * BP), BF16),
    )
    wide = (jax.ShapeDtypeStruct((NB, BP, BP), F32),)
    args = (lists, state) if opening else (lists, state, rb)
    outs = pl.pallas_call(
        functools.partial(local_kernel, opening),
        in_specs=[SMEM] + [VMEM] * (len(args) - 1),
        out_shape=outs + (wide if opening else ()),
        out_specs=(VMEM,) * (3 if opening else 2),
        scratch_shapes=[
            pltpu.VMEM((NB, BP, DEPTH), BF16),
            pltpu.VMEM((NB, 16, 2 * BP), BF16),
            pltpu.VMEM((GROUP, 4 * BP, BP), BF16),
        ],
        compiler_params=PARAMS,
        cost_estimate=cost(10000000000, 3500000, 4000000),
        name="local_pairs",
    )(*args)
    return outs if opening else (*outs, rb)


def ghost_kernel(last, *refs):
    (par_ref, ghost_ref, list_ref, owner_ref), refs = refs[:4], refs[4:]
    (cell_ref, state_ref, near_in, far_in, aux_ref, part_ref, g_ref), refs = refs[:7], refs[7:]
    if last:
        (pos_out, vel_out, keep_ref, give_ref), (*scratch, spread_ref) = refs[:4], refs[4:]
    else:
        (new_ref, near_out, far_out), scratch = refs[:3], refs[3:]
    ext_ref, jt_ref, a_ref, rb_ref, acc_ref = scratch
    par = par_ref[0]
    row = row_index()

    sign = 1.0 - 2.0 * par.astype(F32)
    shift = jnp.where(row[0] == 0, SLAB * sign, 0.0)
    for s in range(NG):
        ext_ref[NG * (1 - par) + s] = near_in[s] + shift
        ext_ref[NG * par + s] = far_in[s] - shift
    for s in range(2 * NG, 8):
        ext_ref[s] = jnp.zeros((8, BP), F32)
    column = jnp.transpose(ext_ref[:, 6, :])
    for b in range(2 * NG):
        rb_ref[b] = jnp.broadcast_to(column[:, b : b + 1], (BP, BP))
    partner_side(ext_ref[0:4], 0, jt_ref, a_ref)
    acc_ref[...] = part_ref[...]
    ghost_loop(list_ref[4 * ROOM + 1], list_ref, acc_ref, state_ref, jt_ref, g_ref, a_ref, rb_ref)

    tile = state_ref[...]
    raw = acc_ref[0:NB]
    acc = jnp.concatenate(
        [
            raw[:, 0:3] + raw[:, 3:6] + raw[:, 6:9],
            raw[:, 16:19] + raw[:, 19:22] + raw[:, 22:25],
            raw[:, 9:10],
            raw[:, 25:26],
        ],
        axis=1,
    )
    aux = aux_ref[...]
    by_x = STIFF * (tile * acc[:, 6:7] - acc)
    by_v = acc - tile * acc[:, 7:8]
    force = swap3(by_x) + by_v
    beta = aux[:, 6:7]
    mass = aux[:, 7:8]
    gravity = jnp.where(row == 5, GRAVITY_Z, 0.0)
    velocity = tile + STEP * ((force + beta * (aux - tile)) / mass + gravity)
    place = tile + STEP * swap3(velocity)
    moved = jnp.where(row < 3, place, jnp.where(row < 6, velocity, tile))

    if not last:
        new_ref[...] = moved
        fill_sends(par_ref, ghost_ref, new_ref, near_out, far_out)
        return

    for b in range(NB):
        lanes = slice(b * BP, (b + 1) * BP)
        pos_out[:, lanes] = moved[b, 0:3]
        vel_out[:, lanes] = moved[b, 3:6]

    keep_ref[...] = jnp.zeros(keep_ref.shape, F32)
    give_ref[...] = jnp.zeros(give_ref.shape, F32)
    drag = beta * moved
    quarter = lax.broadcasted_iota(jnp.int32, (DEPROWS, BP), 0) % CHUNKS
    place_of = lax.broadcasted_iota(jnp.int32, (BP, BP), 0)
    zeros = jnp.zeros((8, BP), F32)
    tail = jnp.zeros((DEPROWS - CHUNKS * K, BP), F32)
    for b in range(NB):
        cell = cell_ref[b : b + 1, :]
        chunk = cell // BP
        hot = jnp.where(place_of == cell % BP, 1.0, 0.0).astype(BF16)
        values = [mass[b], beta[b], drag[b, 3:4], drag[b, 4:5], drag[b, 5:6]]
        amounts = jnp.concatenate([jnp.broadcast_to(v, (CHUNKS, BP)) for v in values] + [tail], axis=0)
        amounts = jnp.where(quarter == chunk, amounts, 0.0)
        stacked = jnp.concatenate(list(parts3(amounts)) + [zeros], axis=0).astype(BF16)
        spread = lax.dot_general(stacked, hot, (((1,), (1,)), ((), ())), preferred_element_type=F32)
        spread_ref[b] = spread[0:DEPROWS] + spread[DEPROWS : 2 * DEPROWS] + spread[2 * DEPROWS : 3 * DEPROWS]

    for b in range(NB):
        owner = owner_ref[b]

        def put(target, b=b, chip=owner // 2):
            for q in range(K):
                target[chip, q] += spread_ref[b, CHUNKS * q : CHUNKS * (q + 1)]

        mine = owner % 2 == par
        pl.when(mine)(functools.partial(put, keep_ref))
        pl.when(jnp.logical_not(mine))(functools.partial(put, give_ref))


def ghost_pairs(last, chips, scalars, cells, state, near, far, aux, part, g):
    tile = jax.ShapeDtypeStruct((NB, 8, BP), F32)
    send = jax.ShapeDtypeStruct((NG, 8, BP), F32)
    if last:
        flat = jax.ShapeDtypeStruct((3, NB * BP), F32)
        dep = jax.ShapeDtypeStruct((chips, K, CHUNKS, BP), F32)
        outs = (flat, flat, dep, dep)
    else:
        outs = (tile, send, send)
    return pl.pallas_call(
        functools.partial(ghost_kernel, last),
        in_specs=[SMEM] * 4 + [VMEM] * 7,
        out_shape=outs,
        out_specs=(VMEM,) * len(outs),
        scratch_shapes=[
            pltpu.VMEM((8, 8, BP), F32),
            pltpu.VMEM((2 * NG, BP, DEPTH), BF16),
            pltpu.VMEM((2 * NG, 16, 2 * BP), BF16),
            pltpu.VMEM((2 * NG, BP, BP), F32),
            pltpu.VMEM((NB + 1, 32, BP), F32),
        ]
        + ([pltpu.VMEM((NB, DEPROWS, BP), F32)] if last else []),
        compiler_params=PARAMS,
        cost_estimate=cost(2000000000, 2000000, 500000),
        name="ghost_pairs_last" if last else "ghost_pairs",
    )(*scalars, cells, state, near, far, aux, part, g)


def known_kernel(dep_ref, gas_ref, void_ref, known_ref, low_ref, high_ref):
    dep = jnp.sum(dep_ref[...], axis=0)
    void = CELL_VOLUME / (CELL_VOLUME + dep[0])
    inertia = RHO_STEP * void
    void_ref[...] = void
    gas = [
        jnp.concatenate([gas_ref[c : c + 1, s * BP : (s + 1) * BP] for s in range(CHUNKS)], axis=0)
        for c in range(3)
    ]
    diag = inertia + dep[1] / CELL_VOLUME + 2.0 * VISCOSITY
    known = [inertia * gas[c] + dep[2 + c] / CELL_VOLUME for c in range(3)]
    for s in range(CHUNKS):
        one = slice(s, s + 1)
        known_ref[s] = jnp.concatenate(
            [g[one] for g in gas] + [k[one] for k in known] + [diag[one], diag[one]], axis=0
        )
    low_ref[...] = known_ref[0]
    high_ref[...] = known_ref[CHUNKS - 1]


def sweeps_kernel(par_ref, near_ref, far_ref, known_ref, gas_out, table_ref):
    odd = par_ref[0] == 1
    below = jnp.where(odd, near_ref[...], far_ref[...])
    above = jnp.where(odd, far_ref[...], near_ref[...])
    full = jnp.concatenate([below] + [known_ref[s] for s in range(CHUNKS)] + [above], axis=1)
    width = full.shape[1]
    inverse = 1.0 / full[6:7]
    pad = jnp.zeros((5, width), F32)
    gas = jnp.concatenate([full[0:3], pad], axis=0)
    known = jnp.concatenate([full[3:6], pad], axis=0)
    for sweep in range(SWEEPS):
        sides = pltpu.roll(gas, 1, 1) + pltpu.roll(gas, width - 1, 1)
        gas = (known + VISCOSITY * sides) * inverse
    gas_out[...] = gas[0:3, BP : BP + CHUNKS * BP]
    for c in range(3):
        for s in range(CHUNKS):
            table_ref[c, s : s + 1, :] = gas[c : c + 1, (s + 1) * BP : (s + 2) * BP]


def pick_kernel(par_ref, owner_ref, cell_ref, mine_ref, other_ref, out_ref):
    par = par_ref[0]
    place_of = lax.broadcasted_iota(jnp.int32, (BP, BP), 0)
    quarter = lax.broadcasted_iota(jnp.int32, (CHUNKS, BP), 0)
    pad = jnp.zeros((4, BP), F32)
    for b in range(NB):
        cell = cell_ref[b : b + 1, :]
        chunk = cell // BP
        hot = jnp.where(place_of == cell % BP, 1.0, 0.0).astype(BF16)
        owner = owner_ref[b]
        chip = owner // 2
        mine = owner % 2 == par
        rows = [jnp.where(mine, mine_ref[chip, c], other_ref[chip, c]) for c in range(3)]
        rows = jnp.concatenate(rows + [pad], axis=0)
        stacked = jnp.concatenate(parts3(rows), axis=0).astype(BF16)
        found = jnp.dot(stacked, hot, preferred_element_type=F32)
        found = found[0:16] + found[16:32] + found[32:48]
        here = quarter == chunk
        out_ref[:, b * BP : (b + 1) * BP] = jnp.concatenate(
            [
                jnp.sum(jnp.where(here, found[4 * c : 4 * c + 4], 0.0), axis=0, keepdims=True)
                for c in range(3)
            ],
            axis=0,
        )


def swap_pairs(count):
    near = [(d, d ^ 1) for d in range(count)]
    far = [(d, (d + 1) % count if d % 2 else (d - 1) % count) for d in range(count)]
    return near, far


def body(
    positions,
    velocities,
    particle_volume,
    drag_coef,
    gas_at_particle,
    pair_first,
    pair_second,
    ghost_list,
    block_owner,
    cell_map,
    gas_velocity,
):
    axes = ("grp", "dom")
    ndom = lax.axis_size("dom")
    near_pairs, far_pairs = swap_pairs(lax.axis_size("grp") * ndom)

    def exchange(near, far):
        far = lax.ppermute(far, axes, far_pairs)
        near = lax.ppermute(near, axes, near_pairs)
        return near, far

    par = (lax.axis_index("dom") & 1).astype(jnp.int32).reshape(1)
    chips = ndom // 2
    same_core = [list(range(core, ndom, 2)) for core in range(2)]
    mass = particle_volume.reshape(NB, BP)
    beta = drag_coef.reshape(NB, BP)
    cells = cell_map.reshape(NB, BP)
    owner = block_owner.reshape(NB)

    state, aux, near, far, lists = prepare(
        par, ghost_list, positions, velocities, gas_at_particle, mass, beta, pair_first, pair_second
    )
    scalars = (par, ghost_list, lists, owner)
    rb = None
    for step in range(SUBSTEPS):
        near, far = exchange(near, far)
        part, g, rb = local_pairs(lists, state, rb)
        last = step == SUBSTEPS - 1
        outs = ghost_pairs(last, chips, scalars, cells, state, near, far, aux, part, g)
        if not last:
            state, near, far = outs
    pos_out, vel_out, keep, give = outs

    dep = keep + lax.ppermute(give, axes, near_pairs)
    dep = lax.all_to_all(dep, "dom", 0, 0, axis_index_groups=same_core, tiled=True)

    tile = jax.ShapeDtypeStruct((8, BP), F32)
    void, known, low, high = pl.pallas_call(
        known_kernel,
        in_specs=[VMEM] * 2,
        out_shape=(
            jax.ShapeDtypeStruct((CHUNKS, BP), F32),
            jax.ShapeDtypeStruct((CHUNKS, 8, BP), F32),
            tile,
            tile,
        ),
        out_specs=(VMEM,) * 4,
        compiler_params=PARAMS,
        cost_estimate=cost(400000, 700000),
        name="known",
    )(dep, gas_velocity)
    odd = par[0] == 1
    near, far = exchange(jnp.where(odd, low, high), jnp.where(odd, high, low))
    gas, table = pl.pallas_call(
        sweeps_kernel,
        in_specs=[SMEM] + [VMEM] * 3,
        out_shape=(
            jax.ShapeDtypeStruct((3, CHUNKS * BP), F32),
            jax.ShapeDtypeStruct((3, CHUNKS, BP), F32),
        ),
        out_specs=(VMEM,) * 2,
        compiler_params=PARAMS,
        cost_estimate=cost(40000, 50000),
        name="sweeps",
    )(par, near, far, known)

    table = jnp.broadcast_to(table[None], (chips, 3, CHUNKS, BP))
    table = lax.all_to_all(table, "dom", 0, 0, axis_index_groups=same_core, tiled=True)
    other = lax.ppermute(table, axes, near_pairs)
    particle_gas = pl.pallas_call(
        pick_kernel,
        in_specs=[SMEM] * 2 + [VMEM] * 3,
        out_shape=jax.ShapeDtypeStruct((3, NB * BP), F32),
        out_specs=VMEM,
        compiler_params=PARAMS,
        cost_estimate=cost(60000000, 900000),
        name="pick",
    )(par, owner, cells, table, other)
    return (pos_out, vel_out, gas, void.reshape(-1), particle_gas)


def solution(mesh):
    both = ("grp", "dom")
    return jax.shard_map(
        body,
        mesh=mesh,
        in_specs=(
            P(None, both),
            P(None, both),
            P(both),
            P(both),
            P(None, both),
            P(both),
            P(both),
            P(None, both),
            P(both, None),
            P(both),
            P(None, both),
        ),
        out_specs=(
            P(None, both),
            P(None, both),
            P(None, both),
            P(both),
            P(None, both),
        ),
        check_vma=False,
    )
```
